32 devices in a mesh: blk: 8 (over z, y), orb: 4 (over x, core).
Axes of the slice: x: 2, y: 2, z: 4, core: 2. Of those that a mesh axis runs over, the one named last changes fastest.
Arguments:
- orbitals: bfloat16 [4096, 8192], P('blk', 'orb'), may hold values from -0.62890625 to 0.62890625
- coulomb_near: bfloat16 [4096, 512], P('blk'), may hold values from -0.52734375 to 0.52734375
- coulomb_far: bfloat16 [4096, 512], P('blk'), may hold values from -0.52734375 to 0.52734375
Outputs:
- exchange: bfloat16 [4096, 8192], P('blk', 'orb')
The draws below stay inside these ranges and needn't reach their ends.
All inputs are finite; a program needn't handle non-finite values.
Results may differ from the reference program's by a relative error of at most 0.0049.
Values may be sent and summed in bfloat16 or wider, within the bound.
No kernel may reach another device: no remote copies, remote signals or barrier semaphores. Data moves between devices by JAX's collectives and lax.ppermute only.
A program may use at most 64 MiB of HBM per device.

```python
import jax
import jax.numpy as jnp

NORB = 8192
BP = 512
NBLK = 8
POINTS = 4096
OFF_FAR = 2


def block_levels(own_key, extent, pieces, smallest, largest):
    level = 1.0
    for position, shards_of in pieces:
        draws = jax.random.uniform(jax.random.fold_in(jax.random.fold_in(own_key, 6), position), (shards_of,), jnp.float32, smallest / len(pieces), largest / len(pieces))
        level = level * jnp.repeat(jnp.exp(draws), extent[position] // shards_of).reshape((-1,) + (1,) * (len(extent) - 1 - position))
    return level


def gaussian(stream_key, dims, deviation, bound, cuts=(), kind=jnp.bfloat16):
    loudness = block_levels(stream_key, dims, cuts, -0.22, 0.18) if cuts else 1.0
    result = jax.random.normal(stream_key, dims, jnp.float32) * deviation * loudness
    return jnp.minimum(jnp.maximum(result, -bound), bound).astype(kind)


def setup_inputs(seed: int = 0) -> dict:
    seeds = jax.random.split(jax.random.key(seed), 4)
    orbitals = gaussian(seeds[0], (POINTS, NORB), (NORB ** -0.25), 0.62890625, ((0, 8), (1, 4)))
    coulomb_near = gaussian(seeds[1], (POINTS, BP), (2 * BP ** -0.5), 0.52734375, ((0, 8),))
    coulomb_far = gaussian(seeds[2], (POINTS, BP), (2 * BP ** -0.5), 0.52734375, ((0, 8),))
    return {"orbitals": orbitals, "coulomb_near": coulomb_near, "coulomb_far": coulomb_far}


def one_offset(blocks, slab, offset):
    partner_vals = jnp.roll(blocks, -offset, axis=0)
    gram = jnp.einsum("bpn,bqn->bpq", blocks.astype(jnp.float32), partner_vals.astype(jnp.float32))
    weighted = (gram * slab.astype(jnp.float32)).astype(jnp.bfloat16)
    own = jnp.einsum("bpq,bqn->bpn", weighted.astype(jnp.float32), partner_vals.astype(jnp.float32))
    part = jnp.einsum("bpq,bpn->bqn", weighted.astype(jnp.float32), blocks.astype(jnp.float32))
    return own + jnp.roll(part, offset, axis=0)


def reference(orbitals, coulomb_near, coulomb_far):
    blocks = orbitals.reshape(NBLK, BP, NORB)
    total = one_offset(blocks, coulomb_near.reshape(NBLK, BP, BP), 1)
    total = total + one_offset(blocks, coulomb_far.reshape(NBLK, BP, BP), OFF_FAR)
    return total.reshape(POINTS, NORB).astype(jnp.bfloat16)
```

```python
import functools

import jax
import jax.numpy as jnp
from jax import lax
from jax.experimental import pallas as pl
from jax.experimental.pallas import tpu as pltpu
from jax.sharding import PartitionSpec as P

MIB = 1024 * 1024
F32, BF16 = jnp.float32, jnp.bfloat16
VMEM = pl.BlockSpec(memory_space=pltpu.VMEM)
ANY = pl.BlockSpec(memory_space=pl.ANY)


def shape(rows, columns, kind):
    return jax.ShapeDtypeStruct((rows, columns), kind)


def cost(flops, moved_bytes):
    return pl.CostEstimate(flops=flops, bytes_accessed=moved_bytes, transcendentals=0)


def outer(left, right):
    return lax.dot_general(left, right, (((1,), (1,)), ((), ())), preferred_element_type=F32)


def inner(left, right):
    return jnp.dot(left, right, preferred_element_type=F32)


def moved(value, axis, pairs):
    return lax.ppermute(value, axis, pairs)


def swapped(value, axis, distance):
    devices = lax.axis_size(axis)
    return lax.ppermute(value, axis, [(i, i ^ distance) for i in range(devices)])


def after(values, *earlier):
    return lax.optimization_barrier((*values, *earlier))[: len(values)]


def quarter_index(distance=0):
    me = lax.axis_index("orb")
    return ((me % 2) * 2 + me // 2) ^ distance


def quarter_rows(rows, distance=0):
    size = rows // 4
    return pl.ds(pl.multiple_of(quarter_index(distance) * size, size), size)


def pack_kernel(x, near, far, near_out, far_out):
    rows, columns = near.shape[0], x.shape[1]
    quarter = rows // 4
    height = rows * quarter // columns
    here = quarter_rows(rows)
    for slab, out in ((far, far_out), (near, near_out)):
        size = out.shape[0] - height
        out[:size, :] = x[:size, :]
        for i in range(rows // height):
            block = slab[i * height : (i + 1) * height, here]
            out[size:, i * quarter : (i + 1) * quarter] = block


def pack(x, near, far, near_size, far_size):
    rows, columns = x.shape
    height = rows * (rows // 4) // columns
    return pl.pallas_call(
        pack_kernel,
        in_specs=[VMEM] * 3,
        out_specs=[VMEM] * 2,
        out_shape=[
            shape(near_size + height, columns, BF16),
            shape(far_size + height, columns, BF16),
        ],
        compiler_params=pltpu.CompilerParams(vmem_limit_bytes=10 * MIB),
        cost_estimate=cost(0, 6 * near_size * columns),
    )(x, near, far)


def unpacked(packed, rows):
    quarter = rows // 4
    height = rows * quarter // packed.shape[1]
    top = packed.shape[0] - height
    blocks = [
        packed[top:, i * quarter : (i + 1) * quarter].astype(F32) for i in range(rows // height)
    ]
    return jnp.concatenate(blocks, 0).T


def gram_first_kernel(x, z, total):
    total[...] = outer(x[...], z[: total.shape[1], :])


def gram_last_kernel(x, y, z, z_more, early, keep, send, late, xy, zy):
    rows, more = x.shape[0], z_more.shape[0]
    size = rows - more
    late[...] = outer(x[...], z_more[...])
    xy[...] = outer(x[...], y[:rows, :])
    zy[:size, :] = outer(z[:size, :], y[:rows, :])
    zy[size:, :] = outer(z_more[...], y[:rows, :])
    quarter = rows // 4
    for distance in range(4):
        target, kind = (keep, F32) if distance < 2 else (send, BF16)
        place = distance % 2 * quarter
        here, there = quarter_rows(rows, distance), slice(place, place + quarter)
        target[there, :rows] = xy[here, :].astype(kind)
        target[there, rows : rows + size] = early[here, :].astype(kind)
        target[there, rows + size : 2 * rows] = late[here, :].astype(kind)
        target[there, 2 * rows :] = zy[here, :].astype(kind)


def gram_first(x, z, size):
    rows, columns = x.shape
    return pl.pallas_call(
        gram_first_kernel,
        in_specs=[VMEM] * 2,
        out_specs=VMEM,
        out_shape=shape(rows, size, F32),
        compiler_params=pltpu.CompilerParams(vmem_limit_bytes=10 * MIB),
        cost_estimate=cost(2 * rows * size * columns, 4 * rows * columns),
    )(x, z)


def gram_last(x, y, z, z_more, early):
    rows, more = x.shape[0], z_more.shape[0]
    return pl.pallas_call(
        gram_last_kernel,
        in_specs=[VMEM] * 5,
        out_specs=[VMEM] * 2,
        out_shape=[shape(rows // 2, 3 * rows, F32), shape(rows // 2, 3 * rows, BF16)],
        scratch_shapes=[pltpu.VMEM((rows, more), F32)] + [pltpu.VMEM((rows, rows), F32)] * 2,
        compiler_params=pltpu.CompilerParams(vmem_limit_bytes=20 * MIB),
        cost_estimate=cost(0, 0),
    )(x, y, z, z_more, early)


def fold_kernel(keep, other, mine, send):
    size = mine.shape[0]
    mine[...] = keep[:size, :] + other[:size, :].astype(F32)
    send[...] = (keep[size:, :] + other[size:, :].astype(F32)).astype(BF16)


def fold(keep, other):
    size, width = keep.shape[0] // 2, keep.shape[1]
    return pl.pallas_call(
        fold_kernel,
        in_specs=[VMEM] * 2,
        out_specs=[VMEM] * 2,
        out_shape=[shape(size, width, F32), shape(size, width, BF16)],
        compiler_params=pltpu.CompilerParams(vmem_limit_bytes=8 * MIB),
        cost_estimate=cost(4 * size * width, 18 * size * width),
    )(keep, other)


def weigh_kernel(mine, other, near, far, near_other, far_other, ahead, xz, zy):
    rows = near.shape[0]
    here = quarter_rows(rows)
    even = lax.axis_index("blk") % 2 == 0
    gram = mine[...] + other[...].astype(F32)
    near_turned, far_turned = unpacked(near_other, rows), unpacked(far_other, rows)
    near_slab = jnp.where(even, near[here, :].astype(F32), near_turned)
    far_slab = jnp.where(even, far[here, :].astype(F32), far_turned)
    ahead[:, :rows] = (gram[:, :rows] * near_slab).astype(BF16)
    weighted = (gram[:, rows : 2 * rows] * far_slab).astype(BF16)
    ahead[:, rows:] = weighted
    xz[...] = weighted
    zy[...] = (gram[:, 2 * rows :] * near_turned).astype(BF16)


def weigh(mine, other, near, far, near_other, far_other):
    size, rows = mine.shape[0], near.shape[0]
    return pl.pallas_call(
        weigh_kernel,
        in_specs=[VMEM] * 6,
        out_specs=[VMEM] * 3,
        out_shape=[shape(size, 2 * rows, BF16), shape(size, rows, BF16), shape(size, rows, BF16)],
        compiler_params=pltpu.CompilerParams(vmem_limit_bytes=8 * MIB),
        cost_estimate=cost(6 * size * rows, 40 * size * rows),
    )(mine, other, near, far, near_other, far_other)


def most_kernel(places, *refs):
    ahead, back, values = refs[:4], refs[4:8], refs[8 : 8 + len(places)]
    out, kept, weights, held, arrived = refs[8 + len(values) :]
    rows, columns = out.shape
    size, tiles, last = rows // 4, 4, kept.shape[1] // 2
    copies = []
    for i, (top, bottom) in enumerate(places):
        source = values[i].at[: bottom - top, :]
        copies.append(pltpu.make_async_copy(source, held.at[top:bottom, :], arrived.at[i]))
        copies[-1].start()

    even = lax.axis_index("blk") % 2 == 0
    for distance in range(4):
        weights[quarter_rows(rows, distance), : 2 * rows] = ahead[distance][...]
    for distance in range(4):
        here = quarter_rows(rows, distance)
        weights[:, pl.ds(pl.multiple_of(3 * rows + here.start, size), size)] = (
            back[distance][:, :rows].astype(F32).T.astype(BF16)
        )
        near = back[distance][:, rows:]

        @pl.when(even)
        def _():
            weights[here, 2 * rows : 3 * rows] = near

        @pl.when(jnp.logical_not(even))
        def _():
            weights[:, pl.ds(pl.multiple_of(2 * rows + here.start, size), size)] = (
                near.astype(F32).T.astype(BF16)
            )

    for i in (2, 3):
        kept[:, (i - 2) * last : (i - 1) * last] = weights[:, i * rows : i * rows + last]
    place = 2 * rows
    for i in (2, 3):
        there = slice(place, place + rows - last)
        weights[:, there] = weights[:, i * rows + last : (i + 1) * rows]
        place += rows - last
    for copy in copies:
        copy.wait()
    for k in range(tiles):
        here = slice(k * columns // tiles, (k + 1) * columns // tiles)
        out[:, here] = inner(weights[:, :place], held[:, here])


def apply_most(places, last, ahead, back, values):
    rows, columns = ahead[0].shape[0] * 4, values[0].shape[1]
    return pl.pallas_call(
        functools.partial(most_kernel, places),
        in_specs=[VMEM] * 8 + [ANY] * len(values),
        out_specs=[VMEM] * 2,
        out_shape=[shape(rows, columns, F32), shape(rows, 2 * last, BF16)],
        scratch_shapes=[
            pltpu.VMEM((rows, 4 * rows), BF16),
            pltpu.VMEM((4 * rows - 2 * last, columns), BF16),
            pltpu.SemaphoreType.DMA((len(values),)),
        ],
        compiler_params=pltpu.CompilerParams(vmem_limit_bytes=22 * MIB),
        cost_estimate=cost(6 * rows * rows * columns, 12 * rows * columns),
    )(*ahead, *back, *values)


def last_kernel(weights, total, u, w, out, result, left):
    rows, columns = out.shape
    last, tiles = u.shape[0], 4
    writes = []
    for k in range(tiles):
        here = slice(k * columns // tiles, (k + 1) * columns // tiles)
        added = inner(weights[:, :last], u[:, here]) + inner(weights[:, last:], w[:, here])
        result[:, here] = (total[:, here] + added).astype(BF16)
        writes.append(pltpu.make_async_copy(result.at[:, here], out.at[:, here], left.at[k]))
        writes[-1].start()
    for write in writes:
        write.wait()


def apply_last(weights, total, u, w):
    rows, columns = total.shape
    last = u.shape[0]
    return pl.pallas_call(
        last_kernel,
        in_specs=[VMEM] * 4,
        out_specs=ANY,
        out_shape=shape(rows, columns, BF16),
        scratch_shapes=[pltpu.VMEM((rows, columns), BF16), pltpu.SemaphoreType.DMA((4,))],
        compiler_params=pltpu.CompilerParams(vmem_limit_bytes=16 * MIB),
        cost_estimate=cost(4 * rows * last * columns, 6 * rows * columns + 4 * last * columns),
    )(weights, total, u, w)


def gather(value):
    by_x = swapped(value, "orb", 2)
    return value, by_x, swapped(value, "orb", 1), swapped(by_x, "orb", 1)


def relayed(x, near, far):
    blocks = lax.axis_size("blk")
    rows, columns = x.shape
    even = lax.axis_index("blk") % 2 == 0
    inward = [(b, (b - 2 if b % 2 == 0 else b + 2) % blocks) for b in range(blocks)]
    outward = [(b, (b + 2 if b % 2 == 0 else b - 2) % blocks) for b in range(blocks)]

    size = rows // 2
    x_half, x_more = x[:size], x[size:]
    near_part, far_part = pack(x, near, far, rows, size)
    y, z = swapped(near_part, "blk", 1), moved(far_part, "blk", inward)
    z_more = moved(x_more, "blk", inward)

    def round_of(zk, xk, *earlier):
        zk, xk = after((zk, xk), *earlier)
        return swapped(zk, "blk", 1), moved(xk, "blk", outward)

    u_more, w_more = round_of(z_more, x_more, z, z_more)

    always = near[0, 0].astype(F32) < 1e30

    def summed(keep, send, near, far, near_part, far_part):
        mine, send = fold(keep, swapped(send, "orb", 1))
        return tuple(weigh(mine, swapped(send, "orb", 2), near, far, near_part, far_part))

    def no_sum(*_):
        return tuple(jnp.zeros((rows // 4, n * rows), BF16) for n in (2, 1, 1))

    keep, send = gram_last(x, y, z, z_more, gram_first(x, z, size))
    ahead, xz, zy = lax.cond(always, summed, no_sum, keep, send, near, far, y, z)
    back_xz = moved(xz, "blk", outward)
    zy_far = moved(zy, "blk", [p for p in outward if p[0] % 2 == 0])
    zy_near = moved(zy, "blk", [(b, b ^ 1) for b in range(0, blocks, 2)])
    u_half, w_half = round_of(z[:size], x_half, back_xz)
    zy_far, zy_near, back_xz = after((zy_far, zy_near, back_xz), u_more, w_more)
    back = gather(jnp.concatenate([back_xz, jnp.where(even, zy_far, zy_near)], 1))

    more = rows - size
    places, place = [], 0
    for height in (rows, size, more, more, more):
        places.append((place, place + height))
        place += height
    values = y, z, z_more, u_more, w_more
    total, weights = apply_most(places, size, gather(ahead), back, values)
    return apply_last(weights, total, u_half, w_half)


def from_behind(value, by):
    devices = lax.axis_size("blk")
    return lax.ppermute(value, "blk", [(i, (i + by) % devices) for i in range(devices)])


def direct(x, near, far, far_offset):
    total = jnp.zeros(x.shape, F32)
    for offset, slab in ((1, near), (far_offset, far)):
        later = from_behind(x, -offset)
        earlier, earlier_slab = from_behind((x, slab), offset)
        for other, scale in ((later, slab), (earlier, earlier_slab.T)):
            gram = lax.psum(outer(x, other), "orb")
            weighted = (gram * scale.astype(F32)).astype(BF16)
            total += inner(weighted, other)
    return total.astype(BF16)


def per_device(orbitals, coulomb_near, coulomb_far):
    far_offset = lax.axis_size("blk") // 4
    if far_offset == 2 and lax.axis_size("orb") == 4:
        return relayed(orbitals, coulomb_near, coulomb_far)
    return direct(orbitals, coulomb_near, coulomb_far, far_offset)


def solution(mesh):
    return jax.shard_map(
        per_device,
        mesh=mesh,
        in_specs=(P("blk", "orb"), P("blk", None), P("blk", None)),
        out_specs=P("blk", "orb"),
        check_vma=False,
    )
```

```python
import functools

import jax
import jax.numpy as jnp
from jax import lax
from jax.experimental import pallas as pl
from jax.experimental.pallas import tpu as pltpu
from jax.sharding import PartitionSpec as P

MIB = 1024 * 1024
F32, BF16 = jnp.float32, jnp.bfloat16
VMEM = pl.BlockSpec(memory_space=pltpu.VMEM)
ANY = pl.BlockSpec(memory_space=pl.ANY)


def shape(rows, columns, kind):
    return jax.ShapeDtypeStruct((rows, columns), kind)


def cost(flops, moved_bytes):
    return pl.CostEstimate(flops=flops, bytes_accessed=moved_bytes, transcendentals=0)


def outer(left, right):
    return lax.dot_general(left, right, (((1,), (1,)), ((), ())), preferred_element_type=F32)


def inner(left, right):
    return jnp.dot(left, right, preferred_element_type=F32)


def moved(value, axis, pairs):
    return lax.ppermute(value, axis, pairs)


def swapped(value, axis, distance):
    devices = lax.axis_size(axis)
    return lax.ppermute(value, axis, [(i, i ^ distance) for i in range(devices)])


def after(values, *earlier):
    return lax.optimization_barrier((*values, *earlier))[: len(values)]


def quarter_index(distance=0):
    me = lax.axis_index("orb")
    return ((me % 2) * 2 + me // 2) ^ distance


def quarter_rows(rows, distance=0):
    size = rows // 4
    return pl.ds(pl.multiple_of(quarter_index(distance) * size, size), size)


def prepare_kernel(x, near, far, upper, lower, near_out, far_out, flag):
    rows = near.shape[0]
    here = quarter_rows(rows)
    upper[...] = x[: upper.shape[0], :]
    lower[...] = x[upper.shape[0] :, :]
    near_out[...] = near[:, here]
    far_out[...] = far[:, here]
    flag[0, 0] = (jnp.max(near[:8, :128].astype(F32)) < 1e30).astype(jnp.int32)


def prepare(x, near, far, first):
    rows, columns = x.shape
    return pl.pallas_call(
        prepare_kernel,
        in_specs=[VMEM] * 3,
        out_specs=[VMEM] * 4 + [pl.BlockSpec(memory_space=pltpu.SMEM)],
        out_shape=[shape(first, columns, BF16), shape(rows - first, columns, BF16)]
        + [shape(rows, rows // 4, BF16)] * 2
        + [shape(1, 1, jnp.int32)],
        compiler_params=pltpu.CompilerParams(vmem_limit_bytes=12 * MIB),
        cost_estimate=cost(0, 6 * rows * columns),
    )(x, near, far)


def gram_kernel(x, y, z, keep, send, total):
    rows = x.shape[0]
    for i, (left, right) in enumerate(((x, y), (x, z), (z, y))):
        total[:, i * rows : (i + 1) * rows] = outer(left[...], right[...])
    quarter = rows // 4
    for distance in range(4):
        target, kind = (keep, F32) if distance < 2 else (send, BF16)
        place = distance % 2 * quarter
        target[place : place + quarter, :] = total[quarter_rows(rows, distance), :].astype(kind)


def gram(x, y, z):
    rows = x.shape[0]
    return pl.pallas_call(
        gram_kernel,
        in_specs=[VMEM] * 3,
        out_specs=[VMEM] * 2,
        out_shape=[shape(rows // 2, 3 * rows, F32), shape(rows // 2, 3 * rows, BF16)],
        scratch_shapes=[pltpu.VMEM((rows, 3 * rows), F32)],
        compiler_params=pltpu.CompilerParams(vmem_limit_bytes=20 * MIB),
        cost_estimate=cost(0, 0),
    )(x, y, z)


def fold_kernel(keep, other, mine, send):
    size = mine.shape[0]
    mine[...] = keep[:size, :] + other[:size, :].astype(F32)
    send[...] = (keep[size:, :] + other[size:, :].astype(F32)).astype(BF16)


def fold(keep, other):
    size, width = keep.shape[0] // 2, keep.shape[1]
    return pl.pallas_call(
        fold_kernel,
        in_specs=[VMEM] * 2,
        out_specs=[VMEM] * 2,
        out_shape=[shape(size, width, F32), shape(size, width, BF16)],
        compiler_params=pltpu.CompilerParams(vmem_limit_bytes=8 * MIB),
        cost_estimate=cost(4 * size * width, 18 * size * width),
    )(keep, other)


def weigh_kernel(mine, other, near, far, near_other, far_other, ahead, xz, zy):
    rows = near.shape[0]
    here = quarter_rows(rows)
    even = lax.axis_index("blk") % 2 == 0
    gram = mine[...] + other[...].astype(F32)
    near_turned = near_other[...].astype(F32).T
    far_turned = far_other[...].astype(F32).T
    near_slab = jnp.where(even, near[here, :].astype(F32), near_turned)
    far_slab = jnp.where(even, far[here, :].astype(F32), far_turned)
    ahead[:, :rows] = (gram[:, :rows] * near_slab).astype(BF16)
    weighted = (gram[:, rows : 2 * rows] * far_slab).astype(BF16)
    ahead[:, rows:] = weighted
    xz[...] = weighted
    zy[...] = (gram[:, 2 * rows :] * near_turned).astype(BF16)


def weigh(mine, other, near, far, near_other, far_other):
    size, rows = mine.shape[0], near.shape[0]
    return pl.pallas_call(
        weigh_kernel,
        in_specs=[VMEM] * 6,
        out_specs=[VMEM] * 3,
        out_shape=[shape(size, 2 * rows, BF16), shape(size, rows, BF16), shape(size, rows, BF16)],
        compiler_params=pltpu.CompilerParams(vmem_limit_bytes=8 * MIB),
        cost_estimate=cost(6 * size * rows, 40 * size * rows),
    )(mine, other, near, far, near_other, far_other)


def most_kernel(places, firsts, *refs):
    ahead, back, values = refs[:4], refs[4:8], refs[8 : 8 + len(places)]
    out, kept, weights, held, arrived = refs[8 + len(values) :]
    rows, columns = out.shape
    size, tiles = rows // 4, 4
    copies = []
    for i, (start, stop) in enumerate(places):
        source = values[i].at[: stop - start, :]
        copies.append(pltpu.make_async_copy(source, held.at[start:stop, :], arrived.at[i]))
        copies[-1].start()

    even = lax.axis_index("blk") % 2 == 0
    for distance in range(4):
        weights[quarter_rows(rows, distance), : 2 * rows] = ahead[distance][...]
    for distance in range(4):
        here = quarter_rows(rows, distance)
        weights[:, pl.ds(pl.multiple_of(3 * rows + here.start, size), size)] = (
            back[distance][:, :rows].astype(F32).T.astype(BF16)
        )
        near = back[distance][:, rows:]

        @pl.when(even)
        def _():
            weights[here, 2 * rows : 3 * rows] = near

        @pl.when(jnp.logical_not(even))
        def _():
            weights[:, pl.ds(pl.multiple_of(2 * rows + here.start, size), size)] = (
                near.astype(F32).T.astype(BF16)
            )

    put, place = 0, 2 * rows
    for i, first in zip((2, 3), firsts):
        kept[:, put : put + first] = weights[:, i * rows : i * rows + first]
        there = slice(place, place + rows - first)
        weights[:, there] = weights[:, i * rows + first : (i + 1) * rows]
        put, place = put + first, place + rows - first
    for copy in copies:
        copy.wait()
    for k in range(tiles):
        here = slice(k * columns // tiles, (k + 1) * columns // tiles)
        out[:, here] = inner(weights[:, :place], held[:, here])


def apply_most(places, firsts, ahead, back, values):
    rows, columns = ahead[0].shape[0] * 4, values[0].shape[1]
    return pl.pallas_call(
        functools.partial(most_kernel, places, firsts),
        in_specs=[VMEM] * 8 + [ANY] * len(values),
        out_specs=[VMEM] * 2,
        out_shape=[shape(rows, columns, F32), shape(rows, sum(firsts), BF16)],
        scratch_shapes=[
            pltpu.VMEM((rows, 4 * rows), BF16),
            pltpu.VMEM((4 * rows - sum(firsts), columns), BF16),
            pltpu.SemaphoreType.DMA((len(values),)),
        ],
        compiler_params=pltpu.CompilerParams(vmem_limit_bytes=22 * MIB),
        cost_estimate=cost(0, 0),
    )(*ahead, *back, *values)


def last_kernel(weights, total, u, w, out, result, left):
    rows, columns = out.shape
    last, tiles = u.shape[0], 4
    writes = []
    for k in range(tiles):
        here = slice(k * columns // tiles, (k + 1) * columns // tiles)
        added = inner(weights[:, :last], u[:, here]) + inner(weights[:, last:], w[:, here])
        result[:, here] = (total[:, here] + added).astype(BF16)
        writes.append(pltpu.make_async_copy(result.at[:, here], out.at[:, here], left.at[k]))
        writes[-1].start()
    for write in writes:
        write.wait()


def apply_last(weights, total, u, w):
    rows, columns = total.shape
    last = (u.shape[0] + w.shape[0]) // 2
    return pl.pallas_call(
        last_kernel,
        in_specs=[VMEM] * 4,
        out_specs=ANY,
        out_shape=shape(rows, columns, BF16),
        scratch_shapes=[pltpu.VMEM((rows, columns), BF16), pltpu.SemaphoreType.DMA((4,))],
        compiler_params=pltpu.CompilerParams(vmem_limit_bytes=16 * MIB),
        cost_estimate=cost(4 * rows * last * columns, 6 * rows * columns + 4 * last * columns),
    )(weights, total, u, w)


def merge_kernel(xz, zy_far, zy_near, out):
    rows = xz.shape[1]
    even = lax.axis_index("blk") % 2 == 0
    out[:, :rows] = xz[...]

    @pl.when(even)
    def _():
        out[:, rows:] = zy_far[...]

    @pl.when(jnp.logical_not(even))
    def _():
        out[:, rows:] = zy_near[...]


def merge(xz, zy_far, zy_near):
    size, rows = xz.shape
    return pl.pallas_call(
        merge_kernel,
        in_specs=[VMEM] * 3,
        out_specs=VMEM,
        out_shape=shape(size, 2 * rows, BF16),
        compiler_params=pltpu.CompilerParams(vmem_limit_bytes=4 * MIB),
        cost_estimate=cost(0, 0),
    )(xz, zy_far, zy_near)


def gather(value):
    by_x = swapped(value, "orb", 2)
    return value, by_x, swapped(value, "orb", 1), swapped(by_x, "orb", 1)


def relayed(x, near, far):
    blocks = lax.axis_size("blk")
    rows, columns = x.shape
    inward = [(b, (b - 2 if b % 2 == 0 else b + 2) % blocks) for b in range(blocks)]
    outward = [(b, (b + 2 if b % 2 == 0 else b - 2) % blocks) for b in range(blocks)]

    z, y = moved(x, "blk", inward), swapped(x, "blk", 1)
    size, first = rows // 2, rows // 2 - 16
    x_half, x_more, near_part, far_part, flag = prepare(x, near, far, first)
    near_part = swapped(near_part, "blk", 1)
    far_part = moved(far_part, "blk", [p for p in inward if p[0] % 2])

    zk, xk = after((z, x_more), far_part)
    w_more = moved(xk, "blk", outward)
    u_more = swapped(after((zk[size:],), y, near_part)[0], "blk", 1)

    always = flag[0, 0] == 1

    def summed(keep, send, near, far, near_part, far_part, z):
        mine, send = fold(keep, swapped(send, "orb", 1))
        by_x = swapped(send, "orb", 2)
        return *weigh(mine, by_x, near, far, near_part, far_part), z[:size]

    def no_sum(*_):
        parts = tuple(jnp.zeros((rows // 4, n * rows), BF16) for n in (2, 1, 1))
        return *parts, jnp.zeros((size, columns), BF16)

    keep, send = gram(x, y, z)
    ahead, xz, zy, z_half = lax.cond(
        always, summed, no_sum, keep, send, near, far, near_part, far_part, z
    )
    back_xz = moved(xz, "blk", outward)
    zy_far = moved(zy, "blk", [p for p in outward if p[0] % 2 == 0])
    zy_near = moved(zy, "blk", [(b, b ^ 1) for b in range(0, blocks, 2)])
    zk, xk = after((z_half, x_half), back_xz)
    w_half = moved(xk, "blk", outward)
    zk, ahead = after((zk, ahead), zy_near, zy_far)
    u_half = swapped(zk, "blk", 1)
    zy_far, zy_near, back_xz = after((zy_far, zy_near, back_xz), u_more, w_more)
    back = gather(merge(back_xz, zy_far, zy_near))

    places, place = [], 0
    for height in (rows, rows, rows - size, rows - first):
        places.append((place, place + height))
        place += height
    total, weights = apply_most(places, (size, first), gather(ahead), back, (y, z, u_more, w_more))
    return apply_last(weights, total, u_half, w_half)


def from_behind(value, by):
    devices = lax.axis_size("blk")
    return lax.ppermute(value, "blk", [(i, (i + by) % devices) for i in range(devices)])


def direct(x, near, far, far_offset):
    total = jnp.zeros(x.shape, F32)
    for offset, slab in ((1, near), (far_offset, far)):
        later = from_behind(x, -offset)
        earlier, earlier_slab = from_behind((x, slab), offset)
        for other, scale in ((later, slab), (earlier, earlier_slab.T)):
            gram = lax.psum(outer(x, other), "orb")
            weighted = (gram * scale.astype(F32)).astype(BF16)
            total += inner(weighted, other)
    return total.astype(BF16)


def per_device(orbitals, coulomb_near, coulomb_far):
    far_offset = lax.axis_size("blk") // 4
    if far_offset == 2 and lax.axis_size("orb") == 4:
        return relayed(orbitals, coulomb_near, coulomb_far)
    return direct(orbitals, coulomb_near, coulomb_far, far_offset)


def solution(mesh):
    return jax.shard_map(
        per_device,
        mesh=mesh,
        in_specs=(P("blk", "orb"), P("blk", None), P("blk", None)),
        out_specs=P("blk", "orb"),
        check_vma=False,
    )
```

```python
import functools

import jax
import jax.numpy as jnp
from jax import lax
from jax.experimental import pallas as pl
from jax.experimental.pallas import tpu as pltpu
from jax.sharding import PartitionSpec as P

MIB = 1024 * 1024
SEEN_COST, MOST_COST, SETTLE_COST = 10, 35, 10
F32, BF16 = jnp.float32, jnp.bfloat16
VMEM = pl.BlockSpec(memory_space=pltpu.VMEM)
ANY = pl.BlockSpec(memory_space=pl.ANY)


def shape(rows, columns, kind):
    return jax.ShapeDtypeStruct((rows, columns), kind)


def cost(flops, moved_bytes):
    return pl.CostEstimate(flops=flops, bytes_accessed=moved_bytes, transcendentals=0)


def outer(left, right):
    return lax.dot_general(left, right, (((1,), (1,)), ((), ())), preferred_element_type=F32)


def inner(left, right):
    return jnp.dot(left, right, preferred_element_type=F32)


def moved(value, axis, pairs):
    return lax.ppermute(value, axis, pairs)


def swapped(value, axis, distance):
    devices = lax.axis_size(axis)
    return lax.ppermute(value, axis, [(i, i ^ distance) for i in range(devices)])


def after(values, *earlier):
    return lax.optimization_barrier((*values, *earlier))[: len(values)]


def quarter_index(distance=0):
    me = lax.axis_index("orb")
    return ((me % 2) * 2 + me // 2) ^ distance


def quarter_rows(rows, distance=0):
    size = rows // 4
    return pl.ds(pl.multiple_of(quarter_index(distance) * size, size), size)


def prepare_kernel(x, near, far, upper, lower, near_out, far_out, flag):
    rows = near.shape[0]
    here = quarter_rows(rows)
    upper[...] = x[: upper.shape[0], :]
    lower[...] = x[upper.shape[0] :, :]
    near_out[...] = near[:, here]
    far_out[...] = far[:, here]
    flag[0, 0] = (jnp.max(near[:8, :128].astype(F32)) < 1e30).astype(jnp.int32)


def prepare(x, near, far, first):
    rows, columns = x.shape
    return pl.pallas_call(
        prepare_kernel,
        in_specs=[VMEM] * 3,
        out_specs=[VMEM] * 4 + [pl.BlockSpec(memory_space=pltpu.SMEM)],
        out_shape=[shape(first, columns, BF16), shape(rows - first, columns, BF16)]
        + [shape(rows, rows // 4, BF16)] * 2
        + [shape(1, 1, jnp.int32)],
        compiler_params=pltpu.CompilerParams(vmem_limit_bytes=12 * MIB),
        cost_estimate=cost(0, 6 * rows * columns),
    )(x, near, far)


def gram_kernel(x, y, z, keep, send, total):
    rows = x.shape[0]
    for i, (left, right) in enumerate(((x, y), (x, z), (z, y))):
        total[:, i * rows : (i + 1) * rows] = outer(left[...], right[...])
    quarter = rows // 4
    for distance in range(4):
        target, kind = (keep, F32) if distance < 2 else (send, BF16)
        place = distance % 2 * quarter
        target[place : place + quarter, :] = total[quarter_rows(rows, distance), :].astype(kind)


def gram(x, y, z):
    rows = x.shape[0]
    return pl.pallas_call(
        gram_kernel,
        in_specs=[VMEM] * 3,
        out_specs=[VMEM] * 2,
        out_shape=[shape(rows // 2, 3 * rows, F32), shape(rows // 2, 3 * rows, BF16)],
        scratch_shapes=[pltpu.VMEM((rows, 3 * rows), F32)],
        compiler_params=pltpu.CompilerParams(vmem_limit_bytes=20 * MIB),
        cost_estimate=cost(0, 0),
    )(x, y, z)


def fold_kernel(keep, other, mine, send):
    size = mine.shape[0]
    mine[...] = keep[:size, :] + other[:size, :].astype(F32)
    send[...] = (keep[size:, :] + other[size:, :].astype(F32)).astype(BF16)


def fold(keep, other):
    size, width = keep.shape[0] // 2, keep.shape[1]
    return pl.pallas_call(
        fold_kernel,
        in_specs=[VMEM] * 2,
        out_specs=[VMEM] * 2,
        out_shape=[shape(size, width, F32), shape(size, width, BF16)],
        compiler_params=pltpu.CompilerParams(vmem_limit_bytes=8 * MIB),
        cost_estimate=cost(4 * size * width, 18 * size * width),
    )(keep, other)


def weigh_kernel(mine, other, near, far, near_other, far_other, ahead, pair, xz, zy):
    rows = near.shape[0]
    here = quarter_rows(rows)
    even = lax.axis_index("blk") % 2 == 0
    gram = mine[...] + other[...].astype(F32)
    near_turned = near_other[...].astype(F32).T
    far_turned = far_other[...].astype(F32).T
    near_slab = jnp.where(even, near[here, :].astype(F32), near_turned)
    far_slab = jnp.where(even, far[here, :].astype(F32), far_turned)
    ahead[:, :rows] = (gram[:, :rows] * near_slab).astype(BF16)
    weighted = (gram[:, rows : 2 * rows] * far_slab).astype(BF16)
    ahead[:, rows:] = weighted
    xz[...] = weighted
    pair[:, :rows] = weighted
    weighted = (gram[:, 2 * rows :] * near_turned).astype(BF16)
    pair[:, rows:] = weighted
    zy[...] = weighted


def weigh(mine, other, near, far, near_other, far_other):
    size, rows = mine.shape[0], near.shape[0]
    return pl.pallas_call(
        weigh_kernel,
        in_specs=[VMEM] * 6,
        out_specs=[VMEM] * 4,
        out_shape=[shape(size, n * rows, BF16) for n in (2, 2, 1, 1)],
        compiler_params=pltpu.CompilerParams(vmem_limit_bytes=8 * MIB),
        cost_estimate=cost(6 * size * rows, 40 * size * rows),
    )(mine, other, near, far, near_other, far_other)


def settle_kernel(a0, a1, a2, a3, out):
    for distance, part in enumerate((a0, a1, a2, a3)):
        out[quarter_rows(out.shape[0], distance), :] = part[...]


def settle(parts):
    size, width = parts[0].shape
    return pl.pallas_call(
        settle_kernel,
        in_specs=[VMEM] * 4,
        out_specs=VMEM,
        out_shape=shape(4 * size, width, BF16),
        compiler_params=pltpu.CompilerParams(vmem_limit_bytes=4 * MIB),
        cost_estimate=cost(SETTLE_COST * 10**8, 0),
    )(*parts)


def most_kernel(places, firsts, *refs):
    ahead, back, values = refs[0], refs[1:5], refs[5 : 5 + len(places)]
    out, kept, weights, held, arrived = refs[5 + len(values) :]
    rows, columns = out.shape
    size, tiles = rows // 4, 4
    copies = []
    for i, (start, stop) in enumerate(places):
        source = values[i].at[: stop - start, :]
        copies.append(pltpu.make_async_copy(source, held.at[start:stop, :], arrived.at[i]))
        copies[-1].start()

    even = lax.axis_index("blk") % 2 == 0
    weights[:, : 2 * rows] = ahead[...]
    for distance in range(4):
        here = quarter_rows(rows, distance)
        weights[:, pl.ds(pl.multiple_of(3 * rows + here.start, size), size)] = (
            back[distance][:, :rows].astype(F32).T.astype(BF16)
        )
        near = back[distance][:, rows:]

        @pl.when(even)
        def _():
            weights[here, 2 * rows : 3 * rows] = near

        @pl.when(jnp.logical_not(even))
        def _():
            weights[:, pl.ds(pl.multiple_of(2 * rows + here.start, size), size)] = (
                near.astype(F32).T.astype(BF16)
            )

    put, place = 0, 2 * rows
    for i, first in zip((2, 3), firsts):
        kept[:, put : put + first] = weights[:, i * rows : i * rows + first]
        there = slice(place, place + rows - first)
        weights[:, there] = weights[:, i * rows + first : (i + 1) * rows]
        put, place = put + first, place + rows - first
    for copy in copies:
        copy.wait()
    for k in range(tiles):
        here = slice(k * columns // tiles, (k + 1) * columns // tiles)
        out[:, here] = inner(weights[:, :place], held[:, here])


def apply_most(places, firsts, ahead, back, values):
    rows, columns = values[0].shape
    return pl.pallas_call(
        functools.partial(most_kernel, places, firsts),
        in_specs=[VMEM] * 5 + [ANY] * len(values),
        out_specs=[VMEM] * 2,
        out_shape=[shape(rows, columns, F32), shape(rows, sum(firsts), BF16)],
        scratch_shapes=[
            pltpu.VMEM((rows, 4 * rows), BF16),
            pltpu.VMEM((4 * rows - sum(firsts), columns), BF16),
            pltpu.SemaphoreType.DMA((len(values),)),
        ],
        compiler_params=pltpu.CompilerParams(vmem_limit_bytes=22 * MIB),
        cost_estimate=cost(MOST_COST * 10**8, 0),
    )(ahead, *back, *values)


def last_kernel(weights, total, u, w, _, out, result, left):
    rows, columns = out.shape
    last, tiles = u.shape[0], 4
    writes = []
    for k in range(tiles):
        here = slice(k * columns // tiles, (k + 1) * columns // tiles)
        added = inner(weights[:, :last], u[:, here]) + inner(weights[:, last:], w[:, here])
        result[:, here] = (total[:, here] + added).astype(BF16)
        writes.append(pltpu.make_async_copy(result.at[:, here], out.at[:, here], left.at[k]))
        writes[-1].start()
    for write in writes:
        write.wait()


def apply_last(weights, total, u, w, here):
    rows, columns = total.shape
    last = (u.shape[0] + w.shape[0]) // 2
    return pl.pallas_call(
        last_kernel,
        in_specs=[VMEM] * 4 + [ANY],
        out_specs=ANY,
        out_shape=shape(rows, columns, BF16),
        scratch_shapes=[pltpu.VMEM((rows, columns), BF16), pltpu.SemaphoreType.DMA((4,))],
        compiler_params=pltpu.CompilerParams(vmem_limit_bytes=16 * MIB),
        cost_estimate=cost(4 * rows * last * columns, 6 * rows * columns + 4 * last * columns),
    )(weights, total, u, w, here)


def seen_kernel(value, out):
    out[...] = jnp.ones_like(out)


def seen(value):
    return pl.pallas_call(
        seen_kernel,
        in_specs=[ANY],
        out_specs=VMEM,
        out_shape=shape(8, 128, F32),
        compiler_params=pltpu.CompilerParams(vmem_limit_bytes=MIB),
        cost_estimate=cost(SEEN_COST * 10**8, 0),
    )(value)


def merge_kernel(even_back, odd_back, zy_near, out):
    rows = zy_near.shape[1]
    even = lax.axis_index("blk") % 2 == 0

    @pl.when(even)
    def _():
        out[...] = even_back[...]

    @pl.when(jnp.logical_not(even))
    def _():
        out[:, :rows] = odd_back[...]
        out[:, rows:] = zy_near[...]


def merge(even_back, odd_back, zy_near):
    return pl.pallas_call(
        merge_kernel,
        in_specs=[VMEM] * 3,
        out_specs=VMEM,
        out_shape=shape(*even_back.shape, BF16),
        compiler_params=pltpu.CompilerParams(vmem_limit_bytes=4 * MIB),
        cost_estimate=cost(0, 0),
    )(even_back, odd_back, zy_near)


def gather(value):
    by_x = swapped(value, "orb", 2)
    return value, by_x, swapped(value, "orb", 1), swapped(by_x, "orb", 1)


def relayed(x, near, far):
    blocks = lax.axis_size("blk")
    rows, columns = x.shape
    inward = [(b, (b - 2 if b % 2 == 0 else b + 2) % blocks) for b in range(blocks)]
    outward = [(b, (b + 2 if b % 2 == 0 else b - 2) % blocks) for b in range(blocks)]

    z, y = moved(x, "blk", inward), swapped(x, "blk", 1)
    size, first = rows // 2, rows // 2 - 16
    x_half, x_more, near_part, far_part, flag = prepare(x, near, far, first)
    near_part = swapped(near_part, "blk", 1)
    far_part = moved(far_part, "blk", [p for p in inward if p[0] % 2])

    zk, xk = after((z, x_more), far_part)
    w_more = moved(xk, "blk", outward)
    u_more = swapped(after((zk[size:],), y, near_part)[0], "blk", 1)

    always = flag[0, 0] == 1

    def summed(keep, send, near, far, near_part, far_part, z):
        mine, send = fold(keep, swapped(send, "orb", 1))
        by_x = swapped(send, "orb", 2)
        return *weigh(mine, by_x, near, far, near_part, far_part), z[:size]

    def no_sum(*_):
        parts = tuple(jnp.zeros((rows // 4, n * rows), BF16) for n in (2, 2, 1, 1))
        return *parts, jnp.zeros((size, columns), BF16)

    keep, send = gram(x, y, z)
    ahead, pair, xz, zy, z_half = lax.cond(
        always, summed, no_sum, keep, send, near, far, near_part, far_part, z
    )
    even_back = moved(pair, "blk", [p for p in outward if p[0] % 2 == 0])
    odd_back = moved(xz, "blk", [p for p in outward if p[0] % 2])
    zy_near = moved(zy, "blk", [(b, b ^ 1) for b in range(0, blocks, 2)])
    zk, xk = after((z_half, x_half), xz, w_more)
    w_half = moved(xk, "blk", outward)
    (zk,) = after((zk,), u_more)
    u_half = swapped(zk, "blk", 1)
    ahead = settle(gather(ahead))
    back = after((even_back, odd_back, zy_near), u_more, w_more)
    back = gather(merge(*back))

    places, place = [], 0
    for height in (rows, rows, rows - size, rows - first):
        places.append((place, place + height))
        place += height
    total, weights = apply_most(places, (size, first), ahead, back, (y, z, u_more, w_more))
    return apply_last(weights, total, u_half, w_half, seen(*after((w_half,), total)))


def from_behind(value, by):
    devices = lax.axis_size("blk")
    return lax.ppermute(value, "blk", [(i, (i + by) % devices) for i in range(devices)])


def direct(x, near, far, far_offset):
    total = jnp.zeros(x.shape, F32)
    for offset, slab in ((1, near), (far_offset, far)):
        later = from_behind(x, -offset)
        earlier, earlier_slab = from_behind((x, slab), offset)
        for other, scale in ((later, slab), (earlier, earlier_slab.T)):
            gram = lax.psum(outer(x, other), "orb")
            weighted = (gram * scale.astype(F32)).astype(BF16)
            total += inner(weighted, other)
    return total.astype(BF16)


def per_device(orbitals, coulomb_near, coulomb_far):
    far_offset = lax.axis_size("blk") // 4
    if far_offset == 2 and lax.axis_size("orb") == 4:
        return relayed(orbitals, coulomb_near, coulomb_far)
    return direct(orbitals, coulomb_near, coulomb_far, far_offset)


def solution(mesh):
    return jax.shard_map(
        per_device,
        mesh=mesh,
        in_specs=(P("blk", "orb"), P("blk", None), P("blk", None)),
        out_specs=P("blk", "orb"),
        check_vma=False,
    )
```

```python
import functools

import jax
import jax.numpy as jnp
from jax import lax
from jax.experimental import pallas as pl
from jax.experimental.pallas import tpu as pltpu
from jax.sharding import PartitionSpec as P

MIB = 1024 * 1024
SEEN_COST, MOST_COST, SETTLE_COST = 10, 10, 25
F32, BF16 = jnp.float32, jnp.bfloat16
VMEM = pl.BlockSpec(memory_space=pltpu.VMEM)
ANY = pl.BlockSpec(memory_space=pl.ANY)


def shape(rows, columns, kind):
    return jax.ShapeDtypeStruct((rows, columns), kind)


def cost(flops, moved_bytes):
    return pl.CostEstimate(flops=flops, bytes_accessed=moved_bytes, transcendentals=0)


def outer(left, right):
    return lax.dot_general(left, right, (((1,), (1,)), ((), ())), preferred_element_type=F32)


def inner(left, right):
    return jnp.dot(left, right, preferred_element_type=F32)


def moved(value, axis, pairs):
    return lax.ppermute(value, axis, pairs)


def swapped(value, axis, distance):
    devices = lax.axis_size(axis)
    return lax.ppermute(value, axis, [(i, i ^ distance) for i in range(devices)])


def after(values, *earlier):
    return lax.optimization_barrier((*values, *earlier))[: len(values)]


def quarter_index(distance=0):
    me = lax.axis_index("orb")
    return ((me % 2) * 2 + me // 2) ^ distance


def quarter_rows(rows, distance=0):
    size = rows // 4
    return pl.ds(pl.multiple_of(quarter_index(distance) * size, size), size)


def prepare_kernel(x, near, far, upper, lower, near_out, far_out, flag):
    rows = near.shape[0]
    here = quarter_rows(rows)
    upper[...] = x[: upper.shape[0], :]
    lower[...] = x[upper.shape[0] :, :]
    near_out[...] = near[:, here]
    far_out[...] = far[:, here]
    flag[0, 0] = (jnp.max(near[:8, :128].astype(F32)) < 1e30).astype(jnp.int32)


def prepare(x, near, far, first):
    rows, columns = x.shape
    return pl.pallas_call(
        prepare_kernel,
        in_specs=[VMEM] * 3,
        out_specs=[VMEM] * 4 + [pl.BlockSpec(memory_space=pltpu.SMEM)],
        out_shape=[shape(first, columns, BF16), shape(rows - first, columns, BF16)]
        + [shape(rows, rows // 4, BF16)] * 2
        + [shape(1, 1, jnp.int32)],
        compiler_params=pltpu.CompilerParams(vmem_limit_bytes=12 * MIB),
        cost_estimate=cost(0, 6 * rows * columns),
    )(x, near, far)


def gram_kernel(x, y, z, keep, send, total):
    rows = x.shape[0]
    even = lax.axis_index("blk") % 2 == 0

    @pl.when(even)
    def _():
        total[:, :rows] = outer(z[...], y[...])

    @pl.when(jnp.logical_not(even))
    def _():
        total[:, :rows] = outer(x[...], y[...])

    total[:, rows:] = outer(x[...], z[...])
    quarter = rows // 4
    for distance in range(4):
        target, kind = (keep, F32) if distance < 2 else (send, BF16)
        place = distance % 2 * quarter
        target[place : place + quarter, :] = total[quarter_rows(rows, distance), :].astype(kind)


def gram(x, y, z):
    rows = x.shape[0]
    return pl.pallas_call(
        gram_kernel,
        in_specs=[VMEM] * 3,
        out_specs=[VMEM] * 2,
        out_shape=[shape(rows // 2, 2 * rows, F32), shape(rows // 2, 2 * rows, BF16)],
        scratch_shapes=[pltpu.VMEM((rows, 2 * rows), F32)],
        compiler_params=pltpu.CompilerParams(vmem_limit_bytes=20 * MIB),
        cost_estimate=cost(0, 0),
    )(x, y, z)


def fold_kernel(keep, other, mine, send):
    size = mine.shape[0]
    mine[...] = keep[:size, :] + other[:size, :].astype(F32)
    send[...] = (keep[size:, :] + other[size:, :].astype(F32)).astype(BF16)


def fold(keep, other):
    size, width = keep.shape[0] // 2, keep.shape[1]
    return pl.pallas_call(
        fold_kernel,
        in_specs=[VMEM] * 2,
        out_specs=[VMEM] * 2,
        out_shape=[shape(size, width, F32), shape(size, width, BF16)],
        compiler_params=pltpu.CompilerParams(vmem_limit_bytes=8 * MIB),
        cost_estimate=cost(4 * size * width, 18 * size * width),
    )(keep, other)


def weigh_kernel(mine, other, far, near_other, far_other, pair, xz, by_y):
    rows = far.shape[0]
    even = lax.axis_index("blk") % 2 == 0
    gram = mine[...] + other[...].astype(F32)
    far_turned = far_other[...].astype(F32).T
    far_slab = jnp.where(even, far[quarter_rows(rows), :].astype(F32), far_turned)
    weighted = (gram[:, rows:] * far_slab).astype(BF16)
    xz[...] = weighted
    pair[:, :rows] = weighted
    weighted = (gram[:, :rows] * near_other[...].astype(F32).T).astype(BF16)
    by_y[...] = weighted
    pair[:, rows:] = weighted


def weigh(mine, other, far, near_other, far_other):
    size, rows = mine.shape[0], far.shape[0]
    return pl.pallas_call(
        weigh_kernel,
        in_specs=[VMEM] * 5,
        out_specs=[VMEM] * 3,
        out_shape=[shape(size, n * rows, BF16) for n in (2, 1, 1)],
        compiler_params=pltpu.CompilerParams(vmem_limit_bytes=8 * MIB),
        cost_estimate=cost(6 * size * rows, 40 * size * rows),
    )(mine, other, far, near_other, far_other)


def settle_kernel(a0, a1, a2, a3, out):
    for distance, part in enumerate((a0, a1, a2, a3)):
        out[quarter_rows(out.shape[0], distance), :] = part[...]


def settle(parts):
    size, width = parts[0].shape
    return pl.pallas_call(
        settle_kernel,
        in_specs=[VMEM] * 4,
        out_specs=VMEM,
        out_shape=shape(4 * size, width, BF16),
        compiler_params=pltpu.CompilerParams(vmem_limit_bytes=4 * MIB),
        cost_estimate=cost(SETTLE_COST * 10**8, 0),
    )(*parts)


def most_kernel(places, firsts, *refs):
    ahead, back, values = refs[0], refs[1:5], refs[5 : 5 + len(places)]
    out, kept, weights, held, arrived = refs[5 + len(values) :]
    rows, columns = out.shape
    size, tiles = rows // 4, 4
    copies = []
    for i, (start, stop) in enumerate(places):
        source = values[i].at[: stop - start, :]
        copies.append(pltpu.make_async_copy(source, held.at[start:stop, :], arrived.at[i]))
        copies[-1].start()

    even = lax.axis_index("blk") % 2 == 0
    weights[:, rows : 2 * rows] = ahead[...]
    for distance in range(4):
        here = quarter_rows(rows, distance)
        xw, xu, xy = (back[distance][:, i * rows : (i + 1) * rows] for i in range(3))

        def across(i):
            return pl.ds(pl.multiple_of(i * rows + here.start, size), size)

        weights[:, across(3)] = xw.astype(F32).T.astype(BF16)

        @pl.when(even)
        def _():
            weights[here, 2 * rows : 3 * rows] = xu
            weights[:, across(0)] = xy.astype(F32).T.astype(BF16)

        @pl.when(jnp.logical_not(even))
        def _():
            weights[here, :rows] = xy
            weights[:, across(2)] = xu.astype(F32).T.astype(BF16)

    put, place = 0, 2 * rows
    for i, first in zip((2, 3), firsts):
        kept[:, put : put + first] = weights[:, i * rows : i * rows + first]
        there = slice(place, place + rows - first)
        weights[:, there] = weights[:, i * rows + first : (i + 1) * rows]
        put, place = put + first, place + rows - first
    for copy in copies:
        copy.wait()
    for k in range(tiles):
        here = slice(k * columns // tiles, (k + 1) * columns // tiles)
        out[:, here] = inner(weights[:, :place], held[:, here])


def apply_most(places, firsts, ahead, back, values):
    rows, columns = values[0].shape
    return pl.pallas_call(
        functools.partial(most_kernel, places, firsts),
        in_specs=[VMEM] * 5 + [ANY] * len(values),
        out_specs=[VMEM] * 2,
        out_shape=[shape(rows, columns, F32), shape(rows, sum(firsts), BF16)],
        scratch_shapes=[
            pltpu.VMEM((rows, 4 * rows), BF16),
            pltpu.VMEM((4 * rows - sum(firsts), columns), BF16),
            pltpu.SemaphoreType.DMA((len(values),)),
        ],
        compiler_params=pltpu.CompilerParams(vmem_limit_bytes=22 * MIB),
        cost_estimate=cost(MOST_COST * 10**8, 0),
    )(ahead, *back, *values)


def last_kernel(weights, total, u, w, _, out, result, left):
    rows, columns = out.shape
    last, tiles = u.shape[0], 4
    writes = []
    for k in range(tiles):
        here = slice(k * columns // tiles, (k + 1) * columns // tiles)
        added = inner(weights[:, :last], u[:, here]) + inner(weights[:, last:], w[:, here])
        result[:, here] = (total[:, here] + added).astype(BF16)
        writes.append(pltpu.make_async_copy(result.at[:, here], out.at[:, here], left.at[k]))
        writes[-1].start()
    for write in writes:
        write.wait()


def apply_last(weights, total, u, w, here):
    rows, columns = total.shape
    last = (u.shape[0] + w.shape[0]) // 2
    return pl.pallas_call(
        last_kernel,
        in_specs=[VMEM] * 4 + [ANY],
        out_specs=ANY,
        out_shape=shape(rows, columns, BF16),
        scratch_shapes=[pltpu.VMEM((rows, columns), BF16), pltpu.SemaphoreType.DMA((4,))],
        compiler_params=pltpu.CompilerParams(vmem_limit_bytes=16 * MIB),
        cost_estimate=cost(4 * rows * last * columns, 6 * rows * columns + 4 * last * columns),
    )(weights, total, u, w, here)


def seen_kernel(value, out):
    out[...] = jnp.ones_like(out)


def seen(value):
    return pl.pallas_call(
        seen_kernel,
        in_specs=[ANY],
        out_specs=VMEM,
        out_shape=shape(8, 128, F32),
        compiler_params=pltpu.CompilerParams(vmem_limit_bytes=MIB),
        cost_estimate=cost(SEEN_COST * 10**8, 0),
    )(value)


def merge_kernel(even_back, odd_back, by_y, own, out):
    rows = own.shape[1]
    even = lax.axis_index("blk") % 2 == 0

    @pl.when(even)
    def _():
        out[:, : 2 * rows] = even_back[...]
        out[:, 2 * rows :] = by_y[...]

    @pl.when(jnp.logical_not(even))
    def _():
        out[:, :rows] = odd_back[...]
        out[:, rows : 2 * rows] = by_y[...]
        out[:, 2 * rows :] = own[...]


def merge(even_back, odd_back, by_y, own):
    size, rows = own.shape
    return pl.pallas_call(
        merge_kernel,
        in_specs=[VMEM] * 4,
        out_specs=VMEM,
        out_shape=shape(size, 3 * rows, BF16),
        compiler_params=pltpu.CompilerParams(vmem_limit_bytes=4 * MIB),
        cost_estimate=cost(0, 0),
    )(even_back, odd_back, by_y, own)


def gather(value):
    by_x = swapped(value, "orb", 2)
    return value, by_x, swapped(value, "orb", 1), swapped(by_x, "orb", 1)


def relayed(x, near, far):
    blocks = lax.axis_size("blk")
    rows, columns = x.shape
    inward = [(b, (b - 2 if b % 2 == 0 else b + 2) % blocks) for b in range(blocks)]
    outward = [(b, (b + 2 if b % 2 == 0 else b - 2) % blocks) for b in range(blocks)]

    z, y = moved(x, "blk", inward), swapped(x, "blk", 1)
    size, first = rows // 2, rows // 2 - 16
    x_half, x_more, near_part, far_part, flag = prepare(x, near, far, first)
    near_part = swapped(near_part, "blk", 1)
    far_part = moved(far_part, "blk", [p for p in inward if p[0] % 2])

    zk, xk = after((z, x_more), far_part)
    w_more = moved(xk, "blk", outward)
    u_more = swapped(after((zk[size:],), y, near_part)[0], "blk", 1)

    always = flag[0, 0] == 1

    def summed(keep, send, far, near_part, far_part, z):
        mine, send = fold(keep, swapped(send, "orb", 1))
        by_x = swapped(send, "orb", 2)
        return *weigh(mine, by_x, far, near_part, far_part), z[:size]

    def no_sum(*_):
        parts = tuple(jnp.zeros((rows // 4, n * rows), BF16) for n in (2, 1, 1))
        return *parts, jnp.zeros((size, columns), BF16)

    keep, send = gram(x, y, z)
    pair, xz, own, z_half = lax.cond(always, summed, no_sum, keep, send, far, near_part, far_part, z)
    even_back = moved(pair, "blk", [p for p in outward if p[0] % 2 == 0])
    odd_back = moved(xz, "blk", [p for p in outward if p[0] % 2])
    by_y = swapped(own, "blk", 1)
    zk, xk = after((z_half, x_half), xz, w_more)
    w_half = moved(xk, "blk", outward)
    (zk,) = after((zk,), u_more)
    u_half = swapped(zk, "blk", 1)
    ahead = settle(gather(xz))
    back = after((even_back, odd_back, by_y, own), u_more, w_more)
    back = gather(merge(*back))

    places, place = [], 0
    for height in (rows, rows, rows - size, rows - first):
        places.append((place, place + height))
        place += height
    total, weights = apply_most(places, (size, first), ahead, back, (y, z, u_more, w_more))
    return apply_last(weights, total, u_half, w_half, seen(*after((w_half,), total)))


def from_behind(value, by):
    devices = lax.axis_size("blk")
    return lax.ppermute(value, "blk", [(i, (i + by) % devices) for i in range(devices)])


def direct(x, near, far, far_offset):
    total = jnp.zeros(x.shape, F32)
    for offset, slab in ((1, near), (far_offset, far)):
        later = from_behind(x, -offset)
        earlier, earlier_slab = from_behind((x, slab), offset)
        for other, scale in ((later, slab), (earlier, earlier_slab.T)):
            gram = lax.psum(outer(x, other), "orb")
            weighted = (gram * scale.astype(F32)).astype(BF16)
            total += inner(weighted, other)
    return total.astype(BF16)


def per_device(orbitals, coulomb_near, coulomb_far):
    far_offset = lax.axis_size("blk") // 4
    if far_offset == 2 and lax.axis_size("orb") == 4:
        return relayed(orbitals, coulomb_near, coulomb_far)
    return direct(orbitals, coulomb_near, coulomb_far, far_offset)


def solution(mesh):
    return jax.shard_map(
        per_device,
        mesh=mesh,
        in_specs=(P("blk", "orb"), P("blk", None), P("blk", None)),
        out_specs=P("blk", "orb"),
        check_vma=False,
    )
```

```python
import functools

import jax
import jax.numpy as jnp
from jax import lax
from jax.experimental import pallas as pl
from jax.experimental.pallas import tpu as pltpu
from jax.sharding import PartitionSpec as P

MIB = 1024 * 1024
SEEN_COST, MOST_COST, SETTLE_COST = 10, 10, 25
F32, BF16 = jnp.float32, jnp.bfloat16
VMEM = pl.BlockSpec(memory_space=pltpu.VMEM)
ANY = pl.BlockSpec(memory_space=pl.ANY)


def shape(rows, columns, kind):
    return jax.ShapeDtypeStruct((rows, columns), kind)


def cost(flops, moved_bytes):
    return pl.CostEstimate(flops=flops, bytes_accessed=moved_bytes, transcendentals=0)


def outer(left, right):
    return lax.dot_general(left, right, (((1,), (1,)), ((), ())), preferred_element_type=F32)


def inner(left, right):
    return jnp.dot(left, right, preferred_element_type=F32)


def moved(value, axis, pairs):
    return lax.ppermute(value, axis, pairs)


def swapped(value, axis, distance):
    devices = lax.axis_size(axis)
    return lax.ppermute(value, axis, [(i, i ^ distance) for i in range(devices)])


def after(values, *earlier):
    return lax.optimization_barrier((*values, *earlier))[: len(values)]


def quarter_index(distance=0):
    me = lax.axis_index("orb")
    return ((me % 2) * 2 + me // 2) ^ distance


def quarter_rows(rows, distance=0):
    size = rows // 4
    return pl.ds(pl.multiple_of(quarter_index(distance) * size, size), size)


def prepare_kernel(x, near, far, upper, lower, near_out, far_out, flag):
    rows = near.shape[0]
    here = quarter_rows(rows)
    upper[...] = x[: upper.shape[0], :]
    lower[...] = x[upper.shape[0] :, :]
    near_out[...] = near[:, here]
    far_out[...] = far[:, here]
    flag[0, 0] = (jnp.max(near[:8, :128].astype(F32)) < 1e30).astype(jnp.int32)


def prepare(x, near, far, first):
    rows, columns = x.shape
    return pl.pallas_call(
        prepare_kernel,
        in_specs=[VMEM] * 3,
        out_specs=[VMEM] * 4 + [pl.BlockSpec(memory_space=pltpu.SMEM)],
        out_shape=[shape(first, columns, BF16), shape(rows - first, columns, BF16)]
        + [shape(rows, rows // 4, BF16)] * 2
        + [shape(1, 1, jnp.int32)],
        compiler_params=pltpu.CompilerParams(vmem_limit_bytes=12 * MIB),
        cost_estimate=cost(0, 6 * rows * columns),
    )(x, near, far)


def gram_kernel(x, y, z, keep, send, total):
    rows = x.shape[0]
    even = lax.axis_index("blk") % 2 == 0

    @pl.when(even)
    def _():
        total[:, :rows] = outer(z[...], y[...])

    @pl.when(jnp.logical_not(even))
    def _():
        total[:, :rows] = outer(x[...], y[...])

    total[:, rows:] = outer(x[...], z[...])
    quarter = rows // 4
    for distance in range(4):
        target, kind = (keep, F32) if distance < 2 else (send, BF16)
        place = distance % 2 * quarter
        target[place : place + quarter, :] = total[quarter_rows(rows, distance), :].astype(kind)


def gram(x, y, z):
    rows = x.shape[0]
    return pl.pallas_call(
        gram_kernel,
        in_specs=[VMEM] * 3,
        out_specs=[VMEM] * 2,
        out_shape=[shape(rows // 2, 2 * rows, F32), shape(rows // 2, 2 * rows, BF16)],
        scratch_shapes=[pltpu.VMEM((rows, 2 * rows), F32)],
        compiler_params=pltpu.CompilerParams(vmem_limit_bytes=20 * MIB),
        cost_estimate=cost(0, 0),
    )(x, y, z)


def fold_kernel(keep, other, mine, send):
    size = mine.shape[0]
    mine[...] = keep[:size, :] + other[:size, :].astype(F32)
    send[...] = (keep[size:, :] + other[size:, :].astype(F32)).astype(BF16)


def fold(keep, other):
    size, width = keep.shape[0] // 2, keep.shape[1]
    return pl.pallas_call(
        fold_kernel,
        in_specs=[VMEM] * 2,
        out_specs=[VMEM] * 2,
        out_shape=[shape(size, width, F32), shape(size, width, BF16)],
        compiler_params=pltpu.CompilerParams(vmem_limit_bytes=8 * MIB),
        cost_estimate=cost(4 * size * width, 18 * size * width),
    )(keep, other)


def weigh_kernel(mine, other, far, near_other, far_other, pair, xz, by_y):
    rows = far.shape[0]
    even = lax.axis_index("blk") % 2 == 0
    gram = mine[...] + other[...].astype(F32)
    far_turned = far_other[...].astype(F32).T
    far_slab = jnp.where(even, far[quarter_rows(rows), :].astype(F32), far_turned)
    weighted = (gram[:, rows:] * far_slab).astype(BF16)
    xz[...] = weighted
    pair[:, :rows] = weighted
    weighted = (gram[:, :rows] * near_other[...].astype(F32).T).astype(BF16)
    by_y[...] = weighted
    pair[:, rows:] = weighted


def weigh(mine, other, far, near_other, far_other):
    size, rows = mine.shape[0], far.shape[0]
    return pl.pallas_call(
        weigh_kernel,
        in_specs=[VMEM] * 5,
        out_specs=[VMEM] * 3,
        out_shape=[shape(size, n * rows, BF16) for n in (2, 1, 1)],
        compiler_params=pltpu.CompilerParams(vmem_limit_bytes=8 * MIB),
        cost_estimate=cost(6 * size * rows, 40 * size * rows),
    )(mine, other, far, near_other, far_other)


def settle_kernel(a0, a1, a2, a3, out):
    for distance, part in enumerate((a0, a1, a2, a3)):
        out[quarter_rows(out.shape[0], distance), :] = part[...]


def settle(parts):
    size, width = parts[0].shape
    return pl.pallas_call(
        settle_kernel,
        in_specs=[VMEM] * 4,
        out_specs=VMEM,
        out_shape=shape(4 * size, width, BF16),
        compiler_params=pltpu.CompilerParams(vmem_limit_bytes=4 * MIB),
        cost_estimate=cost(SETTLE_COST * 10**8, 0),
    )(*parts)


def most_kernel(places, firsts, *refs):
    ahead, back, values = refs[0], refs[1:5], refs[5 : 5 + len(places)]
    out, kept, weights, held, arrived = refs[5 + len(values) :]
    rows, columns = out.shape
    size, tiles = rows // 4, 4
    copies = []
    for i, (start, stop) in enumerate(places):
        source = values[i].at[: stop - start, :]
        copies.append(pltpu.make_async_copy(source, held.at[start:stop, :], arrived.at[i]))
        copies[-1].start()

    even = lax.axis_index("blk") % 2 == 0
    weights[:, rows : 2 * rows] = ahead[...]
    for distance in range(4):
        here = quarter_rows(rows, distance)
        xw, xu, xy = (back[distance][:, i * rows : (i + 1) * rows] for i in range(3))

        def across(i):
            return pl.ds(pl.multiple_of(i * rows + here.start, size), size)

        weights[:, across(3)] = xw.astype(F32).T.astype(BF16)

        @pl.when(even)
        def _():
            weights[here, 2 * rows : 3 * rows] = xu
            weights[:, across(0)] = xy.astype(F32).T.astype(BF16)

        @pl.when(jnp.logical_not(even))
        def _():
            weights[here, :rows] = xy
            weights[:, across(2)] = xu.astype(F32).T.astype(BF16)

    put, place = 0, 2 * rows
    for i, first in zip((2, 3), firsts):
        kept[:, put : put + first] = weights[:, i * rows : i * rows + first]
        there = slice(place, place + rows - first)
        weights[:, there] = weights[:, i * rows + first : (i + 1) * rows]
        put, place = put + first, place + rows - first
    for copy in copies:
        copy.wait()
    for k in range(tiles):
        here = slice(k * columns // tiles, (k + 1) * columns // tiles)
        out[:, here] = inner(weights[:, :place], held[:, here])


def apply_most(places, firsts, ahead, back, values):
    rows, columns = values[0].shape
    return pl.pallas_call(
        functools.partial(most_kernel, places, firsts),
        in_specs=[VMEM] * 5 + [ANY] * len(values),
        out_specs=[VMEM] * 2,
        out_shape=[shape(rows, columns, F32), shape(rows, sum(firsts), BF16)],
        scratch_shapes=[
            pltpu.VMEM((rows, 4 * rows), BF16),
            pltpu.VMEM((4 * rows - sum(firsts), columns), BF16),
            pltpu.SemaphoreType.DMA((len(values),)),
        ],
        compiler_params=pltpu.CompilerParams(vmem_limit_bytes=22 * MIB),
        cost_estimate=cost(MOST_COST * 10**8, 0),
    )(ahead, *back, *values)


def last_kernel(weights, total, u, w, _, out, result, left):
    rows, columns = out.shape
    last, tiles = u.shape[0], 8
    writes = []
    for k in range(tiles):
        here = slice(k * columns // tiles, (k + 1) * columns // tiles)
        added = inner(weights[:, :last], u[:, here]) + inner(weights[:, last:], w[:, here])
        result[:, here] = (total[:, here] + added).astype(BF16)
        writes.append(pltpu.make_async_copy(result.at[:, here], out.at[:, here], left.at[k]))
        writes[-1].start()
    for write in writes:
        write.wait()


def apply_last(weights, total, u, w, here):
    rows, columns = total.shape
    last = (u.shape[0] + w.shape[0]) // 2
    return pl.pallas_call(
        last_kernel,
        in_specs=[VMEM] * 4 + [ANY],
        out_specs=ANY,
        out_shape=shape(rows, columns, BF16),
        scratch_shapes=[pltpu.VMEM((rows, columns), BF16), pltpu.SemaphoreType.DMA((8,))],
        compiler_params=pltpu.CompilerParams(vmem_limit_bytes=16 * MIB),
        cost_estimate=cost(4 * rows * last * columns, 6 * rows * columns + 4 * last * columns),
    )(weights, total, u, w, here)


def seen_kernel(value, out):
    out[...] = jnp.ones_like(out)


def seen(value):
    return pl.pallas_call(
        seen_kernel,
        in_specs=[ANY],
        out_specs=VMEM,
        out_shape=shape(8, 128, F32),
        compiler_params=pltpu.CompilerParams(vmem_limit_bytes=MIB),
        cost_estimate=cost(SEEN_COST * 10**8, 0),
    )(value)


def merge_kernel(even_back, odd_back, by_y, own, out):
    rows = own.shape[1]
    even = lax.axis_index("blk") % 2 == 0

    @pl.when(even)
    def _():
        out[:, : 2 * rows] = even_back[...]
        out[:, 2 * rows :] = by_y[...]

    @pl.when(jnp.logical_not(even))
    def _():
        out[:, :rows] = odd_back[...]
        out[:, rows : 2 * rows] = by_y[...]
        out[:, 2 * rows :] = own[...]


def merge(even_back, odd_back, by_y, own):
    size, rows = own.shape
    return pl.pallas_call(
        merge_kernel,
        in_specs=[VMEM] * 4,
        out_specs=VMEM,
        out_shape=shape(size, 3 * rows, BF16),
        compiler_params=pltpu.CompilerParams(vmem_limit_bytes=4 * MIB),
        cost_estimate=cost(0, 0),
    )(even_back, odd_back, by_y, own)


def gather(value):
    by_x = swapped(value, "orb", 2)
    return value, by_x, swapped(value, "orb", 1), swapped(by_x, "orb", 1)


def relayed(x, near, far):
    blocks = lax.axis_size("blk")
    rows, columns = x.shape
    inward = [(b, (b - 2 if b % 2 == 0 else b + 2) % blocks) for b in range(blocks)]
    outward = [(b, (b + 2 if b % 2 == 0 else b - 2) % blocks) for b in range(blocks)]

    z, y = moved(x, "blk", inward), swapped(x, "blk", 1)
    size, first = rows // 2, rows // 2 - 16
    x_half, x_more, near_part, far_part, flag = prepare(x, near, far, first)
    near_part = swapped(near_part, "blk", 1)
    far_part = moved(far_part, "blk", [p for p in inward if p[0] % 2])

    zk, xk = after((z, x_more), far_part)
    w_more = moved(xk, "blk", outward)
    u_more = swapped(after((zk[size:],), y, near_part)[0], "blk", 1)

    always = flag[0, 0] == 1

    def summed(keep, send, far, near_part, far_part, z):
        mine, send = fold(keep, swapped(send, "orb", 1))
        by_x = swapped(send, "orb", 2)
        return *weigh(mine, by_x, far, near_part, far_part), z[:size]

    def no_sum(*_):
        parts = tuple(jnp.zeros((rows // 4, n * rows), BF16) for n in (2, 1, 1))
        return *parts, jnp.zeros((size, columns), BF16)

    keep, send = gram(x, y, z)
    pair, xz, own, z_half = lax.cond(always, summed, no_sum, keep, send, far, near_part, far_part, z)
    even_back = moved(pair, "blk", [p for p in outward if p[0] % 2 == 0])
    odd_back = moved(xz, "blk", [p for p in outward if p[0] % 2])
    by_y = swapped(own, "blk", 1)
    zk, xk = after((z_half, x_half), xz, w_more)
    w_half = moved(xk, "blk", outward)
    (zk,) = after((zk,), u_more)
    u_half = swapped(zk, "blk", 1)
    ahead = settle(gather(xz))
    back = after((even_back, odd_back, by_y, own), u_more, w_more)
    back = gather(merge(*back))

    places, place = [], 0
    for height in (rows, rows, rows - size, rows - first):
        places.append((place, place + height))
        place += height
    total, weights = apply_most(places, (size, first), ahead, back, (y, z, u_more, w_more))
    return apply_last(weights, total, u_half, w_half, seen(*after((w_half,), total)))


def from_behind(value, by):
    devices = lax.axis_size("blk")
    return lax.ppermute(value, "blk", [(i, (i + by) % devices) for i in range(devices)])


def direct(x, near, far, far_offset):
    total = jnp.zeros(x.shape, F32)
    for offset, slab in ((1, near), (far_offset, far)):
        later = from_behind(x, -offset)
        earlier, earlier_slab = from_behind((x, slab), offset)
        for other, scale in ((later, slab), (earlier, earlier_slab.T)):
            gram = lax.psum(outer(x, other), "orb")
            weighted = (gram * scale.astype(F32)).astype(BF16)
            total += inner(weighted, other)
    return total.astype(BF16)


def per_device(orbitals, coulomb_near, coulomb_far):
    far_offset = lax.axis_size("blk") // 4
    if far_offset == 2 and lax.axis_size("orb") == 4:
        return relayed(orbitals, coulomb_near, coulomb_far)
    return direct(orbitals, coulomb_near, coulomb_far, far_offset)


def solution(mesh):
    return jax.shard_map(
        per_device,
        mesh=mesh,
        in_specs=(P("blk", "orb"), P("blk", None), P("blk", None)),
        out_specs=P("blk", "orb"),
        check_vma=False,
    )
```

```python
import functools

import jax
import jax.numpy as jnp
from jax import lax
from jax.experimental import pallas as pl
from jax.experimental.pallas import tpu as pltpu
from jax.sharding import PartitionSpec as P

MIB = 1024 * 1024
SEEN_COST, MOST_COST, SETTLE_COST = 45, 0, 10
F32, BF16 = jnp.float32, jnp.bfloat16
VMEM = pl.BlockSpec(memory_space=pltpu.VMEM)
ANY = pl.BlockSpec(memory_space=pl.ANY)


def shape(rows, columns, kind):
    return jax.ShapeDtypeStruct((rows, columns), kind)


def cost(flops, moved_bytes):
    return pl.CostEstimate(flops=flops, bytes_accessed=moved_bytes, transcendentals=0)


def outer(left, right):
    return lax.dot_general(left, right, (((1,), (1,)), ((), ())), preferred_element_type=F32)


def inner(left, right):
    return jnp.dot(left, right, preferred_element_type=F32)


def moved(value, axis, pairs):
    return lax.ppermute(value, axis, pairs)


def swapped(value, axis, distance):
    devices = lax.axis_size(axis)
    return lax.ppermute(value, axis, [(i, i ^ distance) for i in range(devices)])


def after(values, *earlier):
    return lax.optimization_barrier((*values, *earlier))[: len(values)]


def quarter_index(distance=0):
    me = lax.axis_index("orb")
    return ((me % 2) * 2 + me // 2) ^ distance


def quarter_rows(rows, distance=0):
    size = rows // 4
    return pl.ds(pl.multiple_of(quarter_index(distance) * size, size), size)


def prepare_kernel(x, near, far, left, right, lower, near_out, far_out, flag):
    rows = near.shape[0]
    here = quarter_rows(rows)
    first, half = left.shape
    left[...] = x[:first, :half]
    right[...] = x[:first, half:]
    lower[...] = x[first:, :]
    near_out[...] = near[:, here]
    far_out[...] = far[:, here]
    flag[0, 0] = (jnp.max(near[:8, :128].astype(F32)) < 1e30).astype(jnp.int32)


def prepare(x, near, far, first):
    rows, columns = x.shape
    return pl.pallas_call(
        prepare_kernel,
        in_specs=[VMEM] * 3,
        out_specs=[VMEM] * 5 + [pl.BlockSpec(memory_space=pltpu.SMEM)],
        out_shape=[shape(first, columns // 2, BF16)] * 2
        + [shape(rows - first, columns, BF16)]
        + [shape(rows, rows // 4, BF16)] * 2
        + [shape(1, 1, jnp.int32)],
        compiler_params=pltpu.CompilerParams(vmem_limit_bytes=12 * MIB),
        cost_estimate=cost(0, 6 * rows * columns),
    )(x, near, far)


def gram_kernel(x, y, z, keep, send, total):
    rows = x.shape[0]
    even = lax.axis_index("blk") % 2 == 0

    @pl.when(even)
    def _():
        total[:, :rows] = outer(z[...], y[...])

    @pl.when(jnp.logical_not(even))
    def _():
        total[:, :rows] = outer(x[...], y[...])

    total[:, rows:] = outer(x[...], z[...])
    quarter = rows // 4
    for distance in range(4):
        target, kind = (keep, F32) if distance < 2 else (send, BF16)
        place = distance % 2 * quarter
        target[place : place + quarter, :] = total[quarter_rows(rows, distance), :].astype(kind)


def gram(x, y, z):
    rows = x.shape[0]
    return pl.pallas_call(
        gram_kernel,
        in_specs=[VMEM] * 3,
        out_specs=[VMEM] * 2,
        out_shape=[shape(rows // 2, 2 * rows, F32), shape(rows // 2, 2 * rows, BF16)],
        scratch_shapes=[pltpu.VMEM((rows, 2 * rows), F32)],
        compiler_params=pltpu.CompilerParams(vmem_limit_bytes=20 * MIB),
        cost_estimate=cost(0, 0),
    )(x, y, z)


def fold_kernel(keep, other, mine, send):
    size = mine.shape[0]
    mine[...] = keep[:size, :] + other[:size, :].astype(F32)
    send[...] = (keep[size:, :] + other[size:, :].astype(F32)).astype(BF16)


def fold(keep, other):
    size, width = keep.shape[0] // 2, keep.shape[1]
    return pl.pallas_call(
        fold_kernel,
        in_specs=[VMEM] * 2,
        out_specs=[VMEM] * 2,
        out_shape=[shape(size, width, F32), shape(size, width, BF16)],
        compiler_params=pltpu.CompilerParams(vmem_limit_bytes=8 * MIB),
        cost_estimate=cost(4 * size * width, 18 * size * width),
    )(keep, other)


def weigh_kernel(mine, other, far, near_other, far_other, pair, xz, by_y):
    rows = far.shape[0]
    even = lax.axis_index("blk") % 2 == 0
    gram = mine[...] + other[...].astype(F32)
    far_turned = far_other[...].astype(F32).T
    far_slab = jnp.where(even, far[quarter_rows(rows), :].astype(F32), far_turned)
    weighted = (gram[:, rows:] * far_slab).astype(BF16)
    xz[...] = weighted
    pair[:, :rows] = weighted
    weighted = (gram[:, :rows] * near_other[...].astype(F32).T).astype(BF16)
    by_y[...] = weighted
    pair[:, rows:] = weighted


def weigh(mine, other, far, near_other, far_other):
    size, rows = mine.shape[0], far.shape[0]
    return pl.pallas_call(
        weigh_kernel,
        in_specs=[VMEM] * 5,
        out_specs=[VMEM] * 3,
        out_shape=[shape(size, n * rows, BF16) for n in (2, 1, 1)],
        compiler_params=pltpu.CompilerParams(vmem_limit_bytes=8 * MIB),
        cost_estimate=cost(6 * size * rows, 40 * size * rows),
    )(mine, other, far, near_other, far_other)


def settle_kernel(a0, a1, a2, a3, out):
    for distance, part in enumerate((a0, a1, a2, a3)):
        out[quarter_rows(out.shape[0], distance), :] = part[...]


def settle(parts):
    size, width = parts[0].shape
    return pl.pallas_call(
        settle_kernel,
        in_specs=[VMEM] * 4,
        out_specs=VMEM,
        out_shape=shape(4 * size, width, BF16),
        compiler_params=pltpu.CompilerParams(vmem_limit_bytes=4 * MIB),
        cost_estimate=cost(SETTLE_COST * 10**8, 0),
    )(*parts)


def most_kernel(places, firsts, *refs):
    ahead, back, values = refs[0], refs[1:5], refs[5 : 5 + len(places)]
    out, kept, weights, held, arrived = refs[5 + len(values) :]
    rows, columns = out.shape
    size, tiles = rows // 4, 4
    copies = []
    for i, (start, stop) in enumerate(places):
        source = values[i].at[: stop - start, :]
        copies.append(pltpu.make_async_copy(source, held.at[start:stop, :], arrived.at[i]))
        copies[-1].start()

    even = lax.axis_index("blk") % 2 == 0
    weights[:, rows : 2 * rows] = ahead[...]
    for distance in range(4):
        here = quarter_rows(rows, distance)
        xw, xu, xy = (back[distance][:, i * rows : (i + 1) * rows] for i in range(3))

        def across(i):
            return pl.ds(pl.multiple_of(i * rows + here.start, size), size)

        weights[:, across(3)] = xw.astype(F32).T.astype(BF16)

        @pl.when(even)
        def _():
            weights[here, 2 * rows : 3 * rows] = xu
            weights[:, across(0)] = xy.astype(F32).T.astype(BF16)

        @pl.when(jnp.logical_not(even))
        def _():
            weights[here, :rows] = xy
            weights[:, across(2)] = xu.astype(F32).T.astype(BF16)

    put, place = 0, 2 * rows
    for i, first in zip((2, 3), firsts):
        kept[:, put : put + first] = weights[:, i * rows : i * rows + first]
        there = slice(place, place + rows - first)
        weights[:, there] = weights[:, i * rows + first : (i + 1) * rows]
        put, place = put + first, place + rows - first
    for copy in copies:
        copy.wait()
    for k in range(tiles):
        here = slice(k * columns // tiles, (k + 1) * columns // tiles)
        out[:, here] = inner(weights[:, :place], held[:, here])


def apply_most(places, firsts, ahead, back, values):
    rows, columns = values[0].shape
    return pl.pallas_call(
        functools.partial(most_kernel, places, firsts),
        in_specs=[VMEM] * 5 + [ANY] * len(values),
        out_specs=[VMEM] * 2,
        out_shape=[shape(rows, columns, F32), shape(rows, sum(firsts), BF16)],
        scratch_shapes=[
            pltpu.VMEM((rows, 4 * rows), BF16),
            pltpu.VMEM((4 * rows - sum(firsts), columns), BF16),
            pltpu.SemaphoreType.DMA((len(values),)),
        ],
        compiler_params=pltpu.CompilerParams(vmem_limit_bytes=22 * MIB),
        cost_estimate=cost(MOST_COST * 10**8, 0),
    )(ahead, *back, *values)


def last_kernel(side, weights, total, u, w, *rest):
    out, result, left = rest[-3:]
    last, width = u.shape
    tiles = 4
    writes = []
    for k in range(tiles):
        here = slice(k * width // tiles, (k + 1) * width // tiles)
        there = slice(side * width + here.start, side * width + here.stop)
        added = inner(weights[:, :last], u[:, here]) + inner(weights[:, last:], w[:, here])
        result[:, here] = (total[:, there] + added).astype(BF16)
        writes.append(pltpu.make_async_copy(result.at[:, here], out.at[:, there], left.at[k]))
        writes[-1].start()
    for write in writes:
        write.wait()


def apply_last(weights, total, u, w, *rest):
    *before, side = rest
    return apply_side(weights, total, u, w, before, side)


def apply_side(weights, total, u, w, before, side):
    rows, columns = total.shape
    last, width = u.shape
    return pl.pallas_call(
        functools.partial(last_kernel, side),
        in_specs=[VMEM] * 4 + [ANY] * len(before),
        out_specs=ANY,
        out_shape=shape(rows, columns, BF16),
        scratch_shapes=[pltpu.VMEM((rows, width), BF16), pltpu.SemaphoreType.DMA((4,))],
        input_output_aliases={4: 0} if side else {},
        compiler_params=pltpu.CompilerParams(vmem_limit_bytes=16 * MIB),
        cost_estimate=cost(4 * rows * last * width, 6 * rows * width + 4 * last * width),
    )(weights, total, u, w, *before)


def seen_kernel(one, other, out):
    out[...] = jnp.ones_like(out)


def seen(one, other):
    return pl.pallas_call(
        seen_kernel,
        in_specs=[ANY] * 2,
        out_specs=VMEM,
        out_shape=shape(8, 128, F32),
        compiler_params=pltpu.CompilerParams(vmem_limit_bytes=MIB),
        cost_estimate=cost(SEEN_COST * 10**8, 0),
    )(one, other)


def merge_kernel(even_back, odd_back, by_y, own, out):
    rows = own.shape[1]
    even = lax.axis_index("blk") % 2 == 0

    @pl.when(even)
    def _():
        out[:, : 2 * rows] = even_back[...]
        out[:, 2 * rows :] = by_y[...]

    @pl.when(jnp.logical_not(even))
    def _():
        out[:, :rows] = odd_back[...]
        out[:, rows : 2 * rows] = by_y[...]
        out[:, 2 * rows :] = own[...]


def merge(even_back, odd_back, by_y, own):
    size, rows = own.shape
    return pl.pallas_call(
        merge_kernel,
        in_specs=[VMEM] * 4,
        out_specs=VMEM,
        out_shape=shape(size, 3 * rows, BF16),
        compiler_params=pltpu.CompilerParams(vmem_limit_bytes=4 * MIB),
        cost_estimate=cost(0, 0),
    )(even_back, odd_back, by_y, own)


def gather(value):
    by_x = swapped(value, "orb", 2)
    return value, by_x, swapped(value, "orb", 1), swapped(by_x, "orb", 1)


def relayed(x, near, far):
    blocks = lax.axis_size("blk")
    rows, columns = x.shape
    inward = [(b, (b - 2 if b % 2 == 0 else b + 2) % blocks) for b in range(blocks)]
    outward = [(b, (b + 2 if b % 2 == 0 else b - 2) % blocks) for b in range(blocks)]

    z, y = moved(x, "blk", inward), swapped(x, "blk", 1)
    size, first = rows // 2, rows // 2 - 16
    x_left, x_right, x_more, near_part, far_part, flag = prepare(x, near, far, first)
    near_part = swapped(near_part, "blk", 1)
    far_part = moved(far_part, "blk", [p for p in inward if p[0] % 2])

    zk, xk = after((z, x_more), far_part)
    w_more = moved(xk, "blk", outward)
    u_more = swapped(after((zk[size:],), y, near_part)[0], "blk", 1)

    always = flag[0, 0] == 1

    def summed(keep, send, far, near_part, far_part, z):
        mine, send = fold(keep, swapped(send, "orb", 1))
        by_x = swapped(send, "orb", 2)
        return *weigh(mine, by_x, far, near_part, far_part), z[:size, : columns // 2], z[:size, columns // 2 :]

    def no_sum(*_):
        parts = tuple(jnp.zeros((rows // 4, n * rows), BF16) for n in (2, 1, 1))
        half = jnp.zeros((size, columns // 2), BF16)
        return *parts, half, half

    keep, send = gram(x, y, z)
    pair, xz, own, z_left, z_right = lax.cond(
        always, summed, no_sum, keep, send, far, near_part, far_part, z
    )
    even_back = moved(pair, "blk", [p for p in outward if p[0] % 2 == 0])
    odd_back = moved(xz, "blk", [p for p in outward if p[0] % 2])
    by_y = swapped(own, "blk", 1)
    xl, xr = after((x_left, x_right), xz, w_more)
    zl, zr = after((z_left, z_right), u_more, w_more)
    w_half = moved(xl, "blk", outward), moved(xr, "blk", outward)
    u_half = swapped(zl, "blk", 1), swapped(zr, "blk", 1)
    ahead = settle(gather(xz))
    back = after((even_back, odd_back, by_y, own), u_more, w_more)
    back = merge(*back)
    by_x = swapped(back, "orb", 2)
    (far_x,) = after((by_x,), w_half[0], u_half[0])
    back = back, by_x, swapped(back, "orb", 1), swapped(far_x, "orb", 1)

    places, place = [], 0
    for height in (rows, rows, rows - size, rows - first):
        places.append((place, place + height))
        place += height
    total, weights = apply_most(places, (size, first), ahead, back, (y, z, u_more, w_more))
    here = jnp.zeros((8, 128), F32)
    out = apply_last(weights, total, u_half[0], w_half[0], here, 0)
    here = seen(*after((w_half[1], u_half[1]), out))
    return apply_last(weights, total, u_half[1], w_half[1], out, here, 1)


def from_behind(value, by):
    devices = lax.axis_size("blk")
    return lax.ppermute(value, "blk", [(i, (i + by) % devices) for i in range(devices)])


def direct(x, near, far, far_offset):
    total = jnp.zeros(x.shape, F32)
    for offset, slab in ((1, near), (far_offset, far)):
        later = from_behind(x, -offset)
        earlier, earlier_slab = from_behind((x, slab), offset)
        for other, scale in ((later, slab), (earlier, earlier_slab.T)):
            gram = lax.psum(outer(x, other), "orb")
            weighted = (gram * scale.astype(F32)).astype(BF16)
            total += inner(weighted, other)
    return total.astype(BF16)


def per_device(orbitals, coulomb_near, coulomb_far):
    far_offset = lax.axis_size("blk") // 4
    if far_offset == 2 and lax.axis_size("orb") == 4:
        return relayed(orbitals, coulomb_near, coulomb_far)
    return direct(orbitals, coulomb_near, coulomb_far, far_offset)


def solution(mesh):
    return jax.shard_map(
        per_device,
        mesh=mesh,
        in_specs=(P("blk", "orb"), P("blk", None), P("blk", None)),
        out_specs=P("blk", "orb"),
        check_vma=False,
    )
```

```python
import functools

import jax
import jax.numpy as jnp
from jax import lax
from jax.experimental import pallas as pl
from jax.experimental.pallas import tpu as pltpu
from jax.sharding import PartitionSpec as P

MIB = 1024 * 1024
SEEN_COST, MOST_COST, SETTLE_COST = 10, 10, 40
F32, BF16 = jnp.float32, jnp.bfloat16
VMEM = pl.BlockSpec(memory_space=pltpu.VMEM)
ANY = pl.BlockSpec(memory_space=pl.ANY)


def shape(rows, columns, kind):
    return jax.ShapeDtypeStruct((rows, columns), kind)


def cost(flops, moved_bytes):
    return pl.CostEstimate(flops=flops, bytes_accessed=moved_bytes, transcendentals=0)


def outer(left, right):
    return lax.dot_general(left, right, (((1,), (1,)), ((), ())), preferred_element_type=F32)


def inner(left, right):
    return jnp.dot(left, right, preferred_element_type=F32)


def moved(value, axis, pairs):
    return lax.ppermute(value, axis, pairs)


def swapped(value, axis, distance):
    devices = lax.axis_size(axis)
    return lax.ppermute(value, axis, [(i, i ^ distance) for i in range(devices)])


def after(values, *earlier):
    return lax.optimization_barrier((*values, *earlier))[: len(values)]


def quarter_index(distance=0):
    me = lax.axis_index("orb")
    return ((me % 2) * 2 + me // 2) ^ distance


def quarter_rows(rows, distance=0):
    size = rows // 4
    return pl.ds(pl.multiple_of(quarter_index(distance) * size, size), size)


def prepare_kernel(x, near, far, upper, lower, near_out, far_out, flag):
    rows = near.shape[0]
    here = quarter_rows(rows)
    upper[...] = x[: upper.shape[0], :]
    lower[...] = x[upper.shape[0] :, :]
    near_out[...] = near[:, here]
    far_out[...] = far[:, here]
    flag[0, 0] = (jnp.max(near[:8, :128].astype(F32)) < 1e30).astype(jnp.int32)


def prepare(x, near, far, first):
    rows, columns = x.shape
    return pl.pallas_call(
        prepare_kernel,
        in_specs=[VMEM] * 3,
        out_specs=[VMEM] * 4 + [pl.BlockSpec(memory_space=pltpu.SMEM)],
        out_shape=[shape(first, columns, BF16), shape(rows - first, columns, BF16)]
        + [shape(rows, rows // 4, BF16)] * 2
        + [shape(1, 1, jnp.int32)],
        compiler_params=pltpu.CompilerParams(vmem_limit_bytes=12 * MIB),
        cost_estimate=cost(0, 6 * rows * columns),
    )(x, near, far)


def gram_kernel(x, y, z, keep, send, total):
    rows = x.shape[0]
    even = lax.axis_index("blk") % 2 == 0

    @pl.when(even)
    def _():
        total[:, :rows] = outer(z[...], y[...])

    @pl.when(jnp.logical_not(even))
    def _():
        total[:, :rows] = outer(x[...], y[...])

    total[:, rows:] = outer(x[...], z[...])
    quarter = rows // 4
    for distance in range(4):
        target, kind = (keep, F32) if distance < 2 else (send, BF16)
        place = distance % 2 * quarter
        target[place : place + quarter, :] = total[quarter_rows(rows, distance), :].astype(kind)


def gram(x, y, z):
    rows = x.shape[0]
    return pl.pallas_call(
        gram_kernel,
        in_specs=[VMEM] * 3,
        out_specs=[VMEM] * 2,
        out_shape=[shape(rows // 2, 2 * rows, F32), shape(rows // 2, 2 * rows, BF16)],
        scratch_shapes=[pltpu.VMEM((rows, 2 * rows), F32)],
        compiler_params=pltpu.CompilerParams(vmem_limit_bytes=20 * MIB),
        cost_estimate=cost(0, 0),
    )(x, y, z)


def fold_kernel(keep, other, mine, send):
    size = mine.shape[0]
    mine[...] = keep[:size, :] + other[:size, :].astype(F32)
    send[...] = (keep[size:, :] + other[size:, :].astype(F32)).astype(BF16)


def fold(keep, other):
    size, width = keep.shape[0] // 2, keep.shape[1]
    return pl.pallas_call(
        fold_kernel,
        in_specs=[VMEM] * 2,
        out_specs=[VMEM] * 2,
        out_shape=[shape(size, width, F32), shape(size, width, BF16)],
        compiler_params=pltpu.CompilerParams(vmem_limit_bytes=8 * MIB),
        cost_estimate=cost(4 * size * width, 18 * size * width),
    )(keep, other)


def weigh_kernel(mine, other, far, near_other, far_other, pair, xz, by_y):
    rows = far.shape[0]
    even = lax.axis_index("blk") % 2 == 0
    gram = mine[...] + other[...].astype(F32)
    far_turned = far_other[...].astype(F32).T
    far_slab = jnp.where(even, far[quarter_rows(rows), :].astype(F32), far_turned)
    weighted = (gram[:, rows:] * far_slab).astype(BF16)
    xz[...] = weighted
    pair[:, :rows] = weighted
    weighted = (gram[:, :rows] * near_other[...].astype(F32).T).astype(BF16)
    by_y[...] = weighted
    pair[:, rows:] = weighted


def weigh(mine, other, far, near_other, far_other):
    size, rows = mine.shape[0], far.shape[0]
    return pl.pallas_call(
        weigh_kernel,
        in_specs=[VMEM] * 5,
        out_specs=[VMEM] * 3,
        out_shape=[shape(size, n * rows, BF16) for n in (2, 1, 1)],
        compiler_params=pltpu.CompilerParams(vmem_limit_bytes=8 * MIB),
        cost_estimate=cost(6 * size * rows, 40 * size * rows),
    )(mine, other, far, near_other, far_other)


def settle_kernel(a0, a1, a2, a3, out):
    for distance, part in enumerate((a0, a1, a2, a3)):
        out[quarter_rows(out.shape[0], distance), :] = part[...]


def settle(parts):
    size, width = parts[0].shape
    return pl.pallas_call(
        settle_kernel,
        in_specs=[VMEM] * 4,
        out_specs=VMEM,
        out_shape=shape(4 * size, width, BF16),
        compiler_params=pltpu.CompilerParams(vmem_limit_bytes=4 * MIB),
        cost_estimate=cost(SETTLE_COST * 10**8, 0),
    )(*parts)


def most_kernel(places, firsts, *refs):
    ahead, back, values = refs[0], refs[1:5], refs[5 : 5 + len(places)]
    out, kept, weights, held, arrived = refs[5 + len(values) :]
    rows, columns = out.shape
    size, tiles = rows // 4, 4
    copies = []
    for i, (start, stop) in enumerate(places):
        source = values[i].at[: stop - start, :]
        copies.append(pltpu.make_async_copy(source, held.at[start:stop, :], arrived.at[i]))
        copies[-1].start()

    even = lax.axis_index("blk") % 2 == 0
    weights[:, rows : 2 * rows] = ahead[...]
    for distance in range(4):
        here = quarter_rows(rows, distance)
        xw, xu, xy = (back[distance][:, i * rows : (i + 1) * rows] for i in range(3))

        def across(i):
            return pl.ds(pl.multiple_of(i * rows + here.start, size), size)

        weights[:, across(3)] = xw.astype(F32).T.astype(BF16)

        @pl.when(even)
        def _():
            weights[here, 2 * rows : 3 * rows] = xu
            weights[:, across(0)] = xy.astype(F32).T.astype(BF16)

        @pl.when(jnp.logical_not(even))
        def _():
            weights[here, :rows] = xy
            weights[:, across(2)] = xu.astype(F32).T.astype(BF16)

    put, place = 0, 2 * rows
    for i, first in zip((2, 3), firsts):
        kept[:, put : put + first] = weights[:, i * rows : i * rows + first]
        there = slice(place, place + rows - first)
        weights[:, there] = weights[:, i * rows + first : (i + 1) * rows]
        put, place = put + first, place + rows - first
    for copy in copies:
        copy.wait()
    for k in range(tiles):
        here = slice(k * columns // tiles, (k + 1) * columns // tiles)
        out[:, here] = inner(weights[:, :place], held[:, here])


def apply_most(places, firsts, ahead, back, values):
    rows, columns = values[0].shape
    return pl.pallas_call(
        functools.partial(most_kernel, places, firsts),
        in_specs=[VMEM] * 5 + [ANY] * len(values),
        out_specs=[VMEM] * 2,
        out_shape=[shape(rows, columns, F32), shape(rows, sum(firsts), BF16)],
        scratch_shapes=[
            pltpu.VMEM((rows, 4 * rows), BF16),
            pltpu.VMEM((4 * rows - sum(firsts), columns), BF16),
            pltpu.SemaphoreType.DMA((len(values),)),
        ],
        compiler_params=pltpu.CompilerParams(vmem_limit_bytes=22 * MIB),
        cost_estimate=cost(MOST_COST * 10**8, 0),
    )(ahead, *back, *values)


def last_kernel(weights, total, u, w, _, out, result, left):
    rows, columns = out.shape
    last, tiles = u.shape[0], 8
    writes = []
    for k in range(tiles):
        here = slice(k * columns // tiles, (k + 1) * columns // tiles)
        added = inner(weights[:, :last], u[:, here]) + inner(weights[:, last:], w[:, here])
        result[:, here] = (total[:, here] + added).astype(BF16)
        writes.append(pltpu.make_async_copy(result.at[:, here], out.at[:, here], left.at[k]))
        writes[-1].start()
    for write in writes:
        write.wait()


def apply_last(weights, total, u, w, here):
    rows, columns = total.shape
    last = (u.shape[0] + w.shape[0]) // 2
    return pl.pallas_call(
        last_kernel,
        in_specs=[VMEM] * 4 + [ANY],
        out_specs=ANY,
        out_shape=shape(rows, columns, BF16),
        scratch_shapes=[pltpu.VMEM((rows, columns), BF16), pltpu.SemaphoreType.DMA((8,))],
        compiler_params=pltpu.CompilerParams(vmem_limit_bytes=16 * MIB),
        cost_estimate=cost(4 * rows * last * columns, 6 * rows * columns + 4 * last * columns),
    )(weights, total, u, w, here)


def seen_kernel(value, out):
    out[...] = jnp.ones_like(out)


def seen(value):
    return pl.pallas_call(
        seen_kernel,
        in_specs=[ANY],
        out_specs=VMEM,
        out_shape=shape(8, 128, F32),
        compiler_params=pltpu.CompilerParams(vmem_limit_bytes=MIB),
        cost_estimate=cost(SEEN_COST * 10**8, 0),
    )(value)


def merge_kernel(even_back, odd_back, by_y, own, out):
    rows = own.shape[1]
    even = lax.axis_index("blk") % 2 == 0

    @pl.when(even)
    def _():
        out[:, : 2 * rows] = even_back[...]
        out[:, 2 * rows :] = by_y[...]

    @pl.when(jnp.logical_not(even))
    def _():
        out[:, :rows] = odd_back[...]
        out[:, rows : 2 * rows] = by_y[...]
        out[:, 2 * rows :] = own[...]


def merge(even_back, odd_back, by_y, own):
    size, rows = own.shape
    return pl.pallas_call(
        merge_kernel,
        in_specs=[VMEM] * 4,
        out_specs=VMEM,
        out_shape=shape(size, 3 * rows, BF16),
        compiler_params=pltpu.CompilerParams(vmem_limit_bytes=4 * MIB),
        cost_estimate=cost(0, 0),
    )(even_back, odd_back, by_y, own)


def gather(value):
    by_x = swapped(value, "orb", 2)
    return value, by_x, swapped(value, "orb", 1), swapped(by_x, "orb", 1)


def relayed(x, near, far):
    blocks = lax.axis_size("blk")
    rows, columns = x.shape
    inward = [(b, (b - 2 if b % 2 == 0 else b + 2) % blocks) for b in range(blocks)]
    outward = [(b, (b + 2 if b % 2 == 0 else b - 2) % blocks) for b in range(blocks)]

    z, y = moved(x, "blk", inward), swapped(x, "blk", 1)
    size, first = rows // 2, rows // 2 - 16
    x_half, x_more, near_part, far_part, flag = prepare(x, near, far, first)
    near_part = swapped(near_part, "blk", 1)
    far_part = moved(far_part, "blk", [p for p in inward if p[0] % 2])

    zk, xk = after((z, x_more), far_part)
    w_more = moved(xk, "blk", outward)
    u_more = swapped(after((zk[size:],), y, near_part)[0], "blk", 1)

    always = flag[0, 0] == 1

    def summed(keep, send, far, near_part, far_part, z):
        mine, send = fold(keep, swapped(send, "orb", 1))
        by_x = swapped(send, "orb", 2)
        return *weigh(mine, by_x, far, near_part, far_part), z[:size]

    def no_sum(*_):
        parts = tuple(jnp.zeros((rows // 4, n * rows), BF16) for n in (2, 1, 1))
        return *parts, jnp.zeros((size, columns), BF16)

    keep, send = gram(x, y, z)
    pair, xz, own, z_half = lax.cond(always, summed, no_sum, keep, send, far, near_part, far_part, z)
    even_back = moved(pair, "blk", [p for p in outward if p[0] % 2 == 0])
    odd_back = moved(xz, "blk", [p for p in outward if p[0] % 2])
    by_y = swapped(own, "blk", 1)
    zk, xk = after((z_half, x_half), xz, w_more)
    w_half = moved(xk, "blk", outward)
    (zk,) = after((zk,), u_more)
    u_half = swapped(zk, "blk", 1)
    ahead = settle(gather(xz))
    back = after((even_back, odd_back, by_y, own), u_more, w_more)
    back = gather(merge(*back))

    places, place = [], 0
    for height in (rows, rows, rows - size, rows - first):
        places.append((place, place + height))
        place += height
    total, weights = apply_most(places, (size, first), ahead, back, (y, z, u_more, w_more))
    return apply_last(weights, total, u_half, w_half, seen(*after((w_half,), total)))


def from_behind(value, by):
    devices = lax.axis_size("blk")
    return lax.ppermute(value, "blk", [(i, (i + by) % devices) for i in range(devices)])


def direct(x, near, far, far_offset):
    total = jnp.zeros(x.shape, F32)
    for offset, slab in ((1, near), (far_offset, far)):
        later = from_behind(x, -offset)
        earlier, earlier_slab = from_behind((x, slab), offset)
        for other, scale in ((later, slab), (earlier, earlier_slab.T)):
            gram = lax.psum(outer(x, other), "orb")
            weighted = (gram * scale.astype(F32)).astype(BF16)
            total += inner(weighted, other)
    return total.astype(BF16)


def per_device(orbitals, coulomb_near, coulomb_far):
    far_offset = lax.axis_size("blk") // 4
    if far_offset == 2 and lax.axis_size("orb") == 4:
        return relayed(orbitals, coulomb_near, coulomb_far)
    return direct(orbitals, coulomb_near, coulomb_far, far_offset)


def solution(mesh):
    return jax.shard_map(
        per_device,
        mesh=mesh,
        in_specs=(P("blk", "orb"), P("blk", None), P("blk", None)),
        out_specs=P("blk", "orb"),
        check_vma=False,
    )
```
